32 devices in a mesh: px: 4 (over y, core), py: 4 (over z), lev: 2 (over x).
Axes of the slice: x: 2, y: 2, z: 4, core: 2. Of those that a mesh axis runs over, the one named last changes fastest.
Arguments:
- tracer: float32 [2, 8, 32, 512], P('lev', None, 'px', 'py'), may hold values from -6 to 6
- node_mass: float32 [2, 32, 512], P('lev', 'px', 'py'), may hold values from 0.5 to 2
- wind_x: float32 [2, 32, 512], P('lev', 'px', 'py'), may hold values from -4 to 4
- wind_y: float32 [2, 32, 512], P('lev', 'px', 'py'), may hold values from -4 to 4
- remap: float32 [2, 2], replicated, may hold values from -4 to 4
Outputs:
- remapped: float32 [2, 8, 32, 512], P(None, 'lev', 'px', 'py')
The draws below stay inside these ranges and needn't reach their ends.
All inputs are finite; a program needn't handle non-finite values.
Results may differ from the reference program's by a relative error of at most 0.0001.
Values sent between devices are 32-bit elements; how exact they have to be, the bound alone decides.
A program may use at most 64 MiB of HBM per device.

```python
import math
import jax
import jax.numpy as jnp
import numpy as np
from jax import lax

GLL_NODES = 4
TRACERS = 8
LEVELS = 2
GRID_X = 32
GRID_Y = 512


def level_of(rng, extent, pieces, least, high):
    def one(position, blocks):
        heights = jax.random.uniform(jax.random.fold_in(jax.random.fold_in(rng, 6), position), (blocks,), jnp.float32, least / len(pieces), high / len(pieces))
        return jnp.repeat(jnp.exp(heights), extent[position] // blocks).reshape((-1,) + (1,) * (len(extent) - position - 1))

    loudness = one(*pieces[0])
    for cut in pieces[1:]:
        loudness = loudness * one(*cut)
    return loudness


def centred(rng, dims, scale, reach, split=(), dtype=jnp.bfloat16):
    gain = level_of(rng, dims, split, -0.22, 0.18) if split else 1.0
    values = jax.random.normal(rng, dims, jnp.float32) * scale * gain
    return jnp.minimum(jnp.maximum(values, -reach), reach).astype(dtype)


def setup_inputs(seed: int = 0) -> dict:
    key_list = jax.random.split(jax.random.key(seed), 6)
    return {
        "tracer": centred(key_list[0], (LEVELS, TRACERS, GRID_X, GRID_Y), 1.0, 6.0, ((0, 2), (2, 4), (3, 4)), jnp.float32),
        "node_mass": jnp.clip(jnp.exp(math.log(2.0) - 1.3862944 * jax.random.uniform(key_list[1], (LEVELS, GRID_X, GRID_Y), jnp.float32) ** level_of(key_list[1], (LEVELS, GRID_X, GRID_Y), ((0, 2), (1, 4), (2, 4)), -0.2, 0.2)), 0.5, 2.0),
        "wind_x": centred(key_list[2], (LEVELS, GRID_X, GRID_Y), 1.0, 4.0, ((0, 2), (1, 4), (2, 4)), jnp.float32),
        "wind_y": centred(key_list[3], (LEVELS, GRID_X, GRID_Y), 1.0, 4.0, ((0, 2), (1, 4), (2, 4)), jnp.float32),
        "remap": centred(key_list[4], (LEVELS, LEVELS), LEVELS ** -0.5, 4.0, (), jnp.float32),
    }


sentinel = 1.0e30
step_size = 0.1
section_weights = ((0.0, 1.0), (0.75, 0.25), (1.0 / 3.0, 2.0 / 3.0))


def derivative_table():
    points = np.array([-1.0, -(5.0 ** -0.5), 5.0 ** -0.5, 1.0])
    number = points.shape[0]
    barycentric = np.array([1.0 / np.prod([points[outer] - points[inner] for inner in range(number) if inner != outer]) for outer in range(number)])
    table = np.zeros((number, number))
    for outer in range(number):
        for inner in range(number):
            if inner != outer:
                table[outer, inner] = barycentric[inner] / barycentric[outer] / (points[outer] - points[inner])
    for outer in range(number):
        table[outer, outer] = -np.sum(table[outer])
    return table


def pair_sum(values, which_axis, cyclic):
    layout = values.shape
    where_at = len(layout) + which_axis
    elements = layout[where_at] // GLL_NODES
    blocked = values.reshape(layout[:where_at] + (elements, GLL_NODES) + layout[where_at + 1:])
    head_nodes = lax.slice_in_dim(blocked, 0, 1, axis=where_at + 1)
    tail_nodes = lax.slice_in_dim(blocked, GLL_NODES - 1, GLL_NODES, axis=where_at + 1)
    middle = lax.slice_in_dim(blocked, 1, GLL_NODES - 1, axis=where_at + 1)
    if cyclic:
        before = jnp.roll(tail_nodes, 1, axis=where_at)
        following = jnp.roll(head_nodes, -1, axis=where_at)
    else:
        zero_slab = jnp.zeros_like(lax.slice_in_dim(tail_nodes, 0, 1, axis=where_at))
        before = jnp.concatenate([zero_slab, lax.slice_in_dim(tail_nodes, 0, elements - 1, axis=where_at)], axis=where_at)
        following = jnp.concatenate([lax.slice_in_dim(head_nodes, 1, elements, axis=where_at), zero_slab], axis=where_at)
    joined = jnp.concatenate([head_nodes + before, middle, tail_nodes + following], axis=where_at + 1)
    return joined.reshape(layout)


def shared(values):
    return pair_sum(pair_sum(values, -2, True), -1, False)


def element_extrema(field):
    layout = field.shape
    blocked = field.reshape(layout[0], layout[1], layout[2] // GLL_NODES, GLL_NODES, layout[3] // GLL_NODES, GLL_NODES)
    return jnp.stack([jnp.min(blocked, axis=(3, 5)), -jnp.max(blocked, axis=(3, 5))])


def neighbourhood(padded):
    rows_min = jnp.minimum(jnp.minimum(padded[..., :-2, :], padded[..., 1:-1, :]), padded[..., 2:, :])
    return jnp.minimum(jnp.minimum(rows_min[..., :-2], rows_min[..., 1:-1]), rows_min[..., 2:])


def bounds(field):
    extrema = element_extrema(field)
    extrema = jnp.concatenate([extrema[..., -1:, :], extrema, extrema[..., :1, :]], axis=-2)
    extrema = jnp.pad(extrema, ((0, 0), (0, 0), (0, 0), (0, 0), (1, 1)), constant_values=sentinel)
    result = neighbourhood(extrema)
    return result[0], -result[1]


def tendency(field, wind_x, wind_y, table):
    layout = field.shape
    flux_x = (wind_x[:, None] * field).reshape(layout[0], layout[1], layout[2] // GLL_NODES, GLL_NODES, layout[3])
    slope_x = jnp.einsum("ij,lcejy->lceiy", table, flux_x, precision=lax.Precision.HIGHEST).reshape(layout)
    flux_y = (wind_y[:, None] * field).reshape(layout[0], layout[1], layout[2], layout[3] // GLL_NODES, GLL_NODES)
    slope_y = jnp.einsum("ij,lcxej->lcxei", table, flux_y, precision=lax.Precision.HIGHEST).reshape(layout)
    return field - step_size * (slope_x + slope_y)


def limit(moved, lower, upper):
    layout = moved.shape
    blocked = moved.reshape(layout[0], layout[1], layout[2] // GLL_NODES, GLL_NODES, layout[3] // GLL_NODES, GLL_NODES)
    clipped = jnp.clip(blocked, lower[:, :, :, None, :, None], upper[:, :, :, None, :, None])
    return clipped.reshape(layout)


def reference(tracer, node_mass, wind_x, wind_y, remap):
    table = jnp.asarray(derivative_table(), jnp.float32)
    mass_sum = shared(node_mass)

    def advance(column):
        start = column[:, None]
        field = start
        for share_start, share_new in section_weights:
            lower, upper = bounds(field)
            limited = limit(tendency(field, wind_x, wind_y, table), lower, upper)
            summed = shared(node_mass[:, None] * limited)
            field = share_start * start + share_new * (summed / mass_sum[:, None])
        return jnp.einsum("ab,bxy->axy", remap, field[:, 0], precision=lax.Precision.HIGHEST)

    columns = lax.map(advance, jnp.moveaxis(tracer, 1, 0))
    return jnp.moveaxis(columns, 0, 1)
```

```python
import functools

import jax
import jax.numpy as jnp
import numpy as np
from jax import lax
from jax.experimental import pallas as pl
from jax.experimental.pallas import tpu as pltpu
from jax.sharding import PartitionSpec as P

GLL_NODES = 4
SECTION_REACH = 2
SLOTS = 64

sentinel = 1e30
step_size = 0.1
section_weights = ((0.0, 1.0), (0.75, 0.25), (1.0 / 3.0, 2.0 / 3.0))
MESH = pl.DeviceIdType.MESH


def derivative_table():
    points = np.array([-1.0, -(5.0 ** (-0.5)), 5.0 ** (-0.5), 1.0])
    number = points.shape[0]
    barycentric = np.array(
        [
            1.0
            / np.prod([points[outer] - points[inner] for inner in range(number) if inner != outer])
            for outer in range(number)
        ]
    )
    table = np.zeros((number, number))
    for outer in range(number):
        for inner in range(number):
            if inner != outer:
                table[outer, inner] = (
                    barycentric[inner] / barycentric[outer] / (points[outer] - points[inner])
                )
    for outer in range(number):
        table[outer, outer] = -np.sum(table[outer])
    return table


def rolled(values, shift, axis):
    size = values.shape[axis]
    shift %= size
    return pltpu.roll(values, shift, axis) if shift else values


def moved_by_table(values, table):
    rows = values.shape[0]
    high = values.astype(jnp.bfloat16)
    rest = values - high.astype(jnp.float32)
    middle = rest.astype(jnp.bfloat16)
    low = (rest - middle.astype(jnp.float32)).astype(jnp.bfloat16)
    terms = jnp.dot(
        jnp.concatenate([high, middle, low], axis=0), table, preferred_element_type=jnp.float32
    )
    return terms[:rows] + (terms[rows : 2 * rows] + terms[2 * rows :])


def sections(tracer, node_mass, wind_x, wind_y, inside):
    nodes = range(GLL_NODES)
    table = step_size * derivative_table()

    def node_sums(values):
        first = [values[0][j] + rolled(values[3][j], 1, 0) for j in nodes]
        last = [values[3][j] + rolled(values[0][j], -1, 0) for j in nodes]
        values = [first, values[1], values[2], last]
        return [
            [row[0] + rolled(row[3], 1, 1), row[1], row[2], row[3] + rolled(row[0], -1, 1)]
            for row in values
        ]

    def tree(combine, items):
        while len(items) > 1:
            items = [combine(*items[i : i + 2]) for i in range(0, len(items), 2)]
        return items[0]

    def around(combine, values):
        for axis in (0, 1):
            values = combine(
                combine(values, rolled(values, 1, axis)), rolled(values, -1, axis)
            )
        return values

    inverse = [
        [1.0 / jnp.where(inside, entry, 1.0) for entry in row] for row in node_sums(node_mass)
    ]
    field = tracer
    for share_start, share_new in section_weights:
        flat = [field[i][j] for i in nodes for j in nodes]
        lower = around(jnp.minimum, jnp.where(inside, tree(jnp.minimum, flat), sentinel))
        upper = around(jnp.maximum, jnp.where(inside, tree(jnp.maximum, flat), -sentinel))
        flux_x = [[wind_x[i][j] * field[i][j] for j in nodes] for i in nodes]
        flux_y = [[wind_y[i][j] * field[i][j] for j in nodes] for i in nodes]
        weighted = []
        for i in nodes:
            row = []
            for j in nodes:
                slope_x = tree(jnp.add, [float(table[i, k]) * flux_x[k][j] for k in nodes])
                slope_y = tree(jnp.add, [float(table[j, k]) * flux_y[i][k] for k in nodes])
                moved = field[i][j] - (slope_x + slope_y)
                limited = jnp.minimum(jnp.maximum(moved, lower), upper)
                row.append(node_mass[i][j] * limited)
            weighted.append(row)
        summed = node_sums(weighted)
        field = [
            [
                share_new * (summed[i][j] * inverse[i][j])
                + (share_start * tracer[i][j] if share_start else 0.0)
                for j in nodes
            ]
            for i in nodes
        ]
    return field


def kernel(
    n,
    nz,
    nlev,
    tracer_hbm,
    mass_hbm,
    wind_x_hbm,
    wind_y_hbm,
    remap,
    out,
    tracer_in,
    metric_in,
    blocks_out,
    halos_out,
    blocks,
    halos,
    spread,
    gather,
    results_out,
    results,
    in_sem,
    block_send,
    block_recv,
    halo_send,
    halo_recv,
    result_send,
    result_recv,
):
    tracers, nx, ny = tracer_in.shape
    held = tracers // n
    fields = held + 3
    half = n // nlev
    reach = SECTION_REACH * len(section_weights)
    width = reach * GLL_NODES
    elements_y = ny // GLL_NODES
    elements_x = n * nx // GLL_NODES
    lanes = spread.shape[1] // GLL_NODES
    px, py, lev = lax.axis_index("px"), lax.axis_index("py"), lax.axis_index("lev")
    has_low, has_high = py > 0, py < nz - 1
    target_lev = px // half

    def others(number):
        return [lax.rem(px + d, n) for d in range(number)]

    barrier = pltpu.get_barrier_semaphore()

    def greet(x, y, level):
        pl.semaphore_signal(barrier, inc=1, device_id=(x, y, level), device_id_type=MESH)

    for d, x in enumerate(others(n)):
        pl.when(has_low)(functools.partial(greet, x, py - 1, lev))
        pl.when(has_high)(functools.partial(greet, x, py + 1, lev))
        for step in range(nlev):
            if d or step:
                greet(x, py, lax.rem(lev + step, nlev))

    copies = [pltpu.make_async_copy(tracer_hbm.at[0], tracer_in, in_sem.at[0])]
    for k, source in enumerate((mass_hbm, wind_x_hbm, wind_y_hbm)):
        copies.append(pltpu.make_async_copy(source.at[0], metric_in.at[k], in_sem.at[k + 1]))
    for copy in copies:
        copy.start()
    for copy in copies:
        copy.wait()

    lane = lax.broadcasted_iota(jnp.int32, (nx, halos.shape[2]), 1)

    def halo_tile(group, side):
        tile = jnp.zeros(lane.shape, jnp.float32)
        for k in range(fields):
            piece = tracer_in[group * held + k] if k < held else metric_in[k - held]
            shift = width * k - (ny - width if side else 0)
            wanted = (lane >= width * k) & (lane < width * (k + 1))
            tile = jnp.where(wanted, rolled(piece, shift, 1), tile)
        return tile

    for group in range(n):
        blocks_out[group, :held] = tracer_in[group * held : (group + 1) * held]
        blocks_out[group, held:] = metric_in[...]
        for side in range(2):
            halos_out[side, group] = halo_tile(group, side)

    peers = n * nlev - 1
    pl.semaphore_wait(
        barrier, peers + n * (has_low.astype(jnp.int32) + has_high.astype(jnp.int32))
    )

    mine = pl.ds(pl.multiple_of(px * nx, nx), nx)

    def block_copy(x):
        return pltpu.make_async_remote_copy(
            src_ref=blocks_out.at[x],
            dst_ref=blocks.at[:, mine, :],
            send_sem=block_send.at[x],
            recv_sem=block_recv.at[px],
            device_id=(x, py, lev),
            device_id_type=MESH,
        )

    def halo_copy(x, side):
        return pltpu.make_async_remote_copy(
            src_ref=halos_out.at[side, x],
            dst_ref=halos.at[side, mine, :],
            send_sem=halo_send.at[side, x],
            recv_sem=halo_recv.at[side, px],
            device_id=(x, py + (1 if side else -1), lev),
            device_id_type=MESH,
        )

    sides = ((0, has_low, has_high), (1, has_high, has_low))
    for x in others(n)[1:]:
        block_copy(x).start()
    for side, sends, _ in sides:
        for x in others(n):

            @pl.when(sends)
            def _(side=side, x=x):
                halo_copy(x, side).start()

    blocks[:, mine, :] = blocks_out[px]
    for side, _, gets in sides:

        @pl.when(jnp.logical_not(gets))
        def _(side=side):
            halos[side] = jnp.zeros(halos.shape[1:], jnp.float32)

    def node_of(shape, axis):
        return lax.broadcasted_iota(jnp.int32, shape, axis)

    depth = ny + halos.shape[2]
    source = node_of((depth, 1), 0)
    slot = jnp.where(
        source < ny + width,
        reach + source // GLL_NODES,
        jnp.where(source < ny + 2 * width, (source - ny - width) // GLL_NODES, -SLOTS * lanes),
    )
    place = lax.rem(source, GLL_NODES) * lanes + slot
    column = node_of((1, spread.shape[1]), 1)
    for k in range(held):
        spread[k * depth : (k + 1) * depth] = jnp.where(
            place + k * SLOTS == column, 1.0, 0.0
        ).astype(jnp.bfloat16)
    source = node_of((gather.shape[0], 1), 0)
    at = lax.rem(source, lanes)
    element = lax.rem(at, SLOTS) - reach
    kept = (element >= 0) & (element < elements_y) & (at // SLOTS < held)
    place = jnp.where(
        kept, at // SLOTS * ny + element * GLL_NODES + source // lanes, -1
    )
    gather[...] = jnp.where(place == node_of((1, gather.shape[1]), 1), 1.0, 0.0).astype(
        jnp.bfloat16
    )

    for x in others(n)[1:]:
        rows = pl.ds(pl.multiple_of(x * nx, nx), nx)
        pltpu.make_async_remote_copy(
            src_ref=blocks_out.at[x],
            dst_ref=blocks.at[:, rows, :],
            send_sem=block_send.at[x],
            recv_sem=block_recv.at[x],
            device_id=(x, py, lev),
            device_id_type=MESH,
        ).wait_recv()
    for side, _, gets in sides:
        for x in others(n):

            @pl.when(gets)
            def _(side=side, x=x):
                rows = pl.ds(pl.multiple_of(x * nx, nx), nx)
                pltpu.make_async_remote_copy(
                    src_ref=halos_out.at[side, x],
                    dst_ref=halos.at[side, rows, :],
                    send_sem=halo_send.at[side, x],
                    recv_sem=halo_recv.at[side, x],
                    device_id=(x, py + (-1 if side else 1), lev),
                    device_id_type=MESH,
                ).wait_recv()

    lane = lax.broadcasted_iota(jnp.int32, (elements_x, halos.shape[2]), 1)

    def operand(k):
        parts = []
        for i in range(GLL_NODES):
            rows = pl.ds(i, elements_x, stride=GLL_NODES)
            high = rolled(halos[0, rows, :], -width * k, 1)
            low = rolled(halos[1, rows, :], width - width * k, 1)
            halo = jnp.where(lane < width, high, jnp.where(lane < 2 * width, low, 0.0))
            parts.append(jnp.concatenate([blocks[k, rows, :], halo], axis=1))
        return jnp.concatenate(parts, axis=0)

    def by_node(values):
        return [
            [
                values[i * elements_x : (i + 1) * elements_x, j * lanes : (j + 1) * lanes]
                for j in range(GLL_NODES)
            ]
            for i in range(GLL_NODES)
        ]

    tracer = by_node(
        moved_by_table(jnp.concatenate([operand(k) for k in range(held)], axis=1), spread[...])
    )
    everywhere = spread[:depth]
    for k in range(1, held):
        everywhere = everywhere + spread[k * depth : (k + 1) * depth]
    metric = moved_by_table(
        jnp.concatenate([operand(held + k) for k in range(3)], axis=0), everywhere
    )
    rows = GLL_NODES * elements_x
    node_mass, wind_x, wind_y = (by_node(metric[k * rows : (k + 1) * rows]) for k in range(3))

    slot = lax.rem(lax.broadcasted_iota(jnp.int32, (elements_x, lanes), 1), SLOTS)
    element = py * elements_y + slot - reach
    inside = (slot < elements_y + 2 * reach) & (element >= 0) & (element < nz * elements_y)
    evolved = sections(tracer, node_mass, wind_x, wind_y, inside)

    evolved = moved_by_table(
        jnp.concatenate([jnp.concatenate(row, axis=1) for row in evolved], axis=0), gather[...]
    )
    for k in range(held):
        for i in range(GLL_NODES):
            results_out[k, pl.ds(i, elements_x, stride=GLL_NODES), :] = evolved[
                i * elements_x : (i + 1) * elements_x, k * ny : (k + 1) * ny
            ]

    def result_copy(x, level, holder, to):
        return pltpu.make_async_remote_copy(
            src_ref=results_out.at[:, pl.ds(pl.multiple_of(x * nx, nx), nx), :],
            dst_ref=results.at[level, pl.ds(holder * held, held)],
            send_sem=result_send.at[x],
            recv_sem=result_recv.at[level, holder],
            device_id=to,
            device_id_type=MESH,
        )

    holder = lax.rem(px, half)
    for d, x in enumerate(others(n)):
        copy = result_copy(x, lev, holder, (x, py, target_lev))
        if d:
            copy.start()
        else:
            pl.when(target_lev != lev)(copy.start)

    @pl.when(target_lev == lev)
    def _():
        results[lev, pl.ds(holder * held, held)] = results_out[:, mine, :]

    for level in range(nlev):
        for j in range(half):
            x = lev * half + j

            @pl.when(jnp.logical_or(x != px, lev != level))
            def _(x=x, level=level, j=j):
                result_copy(px, level, j, (x, py, level)).wait_recv()

    for a in range(nlev):
        total = remap[a, 0] * results[0]
        for b in range(1, nlev):
            total = total + remap[a, b] * results[b]
        out[a] = total

    for x in others(n)[1:]:
        block_copy(x).wait_send()
    for side, sends, _ in sides:
        for x in others(n):

            @pl.when(sends)
            def _(side=side, x=x):
                halo_copy(x, side).wait_send()

    for d, x in enumerate(others(n)):
        copy = result_copy(x, lev, holder, (x, py, target_lev))
        if d:
            copy.wait_send()
        else:
            pl.when(target_lev != lev)(copy.wait_send)


def shards(n, nz, nlev, tracer, node_mass, wind_x, wind_y, remap):
    levels, tracers, nx, ny = tracer.shape
    held = tracers // n
    fields = held + 3
    reach = SECTION_REACH * len(section_weights)
    width = reach * GLL_NODES
    elements_y = ny // GLL_NODES
    if levels != 1 or tracers % n or n % nlev or nx % 8 or ny % 128:
        raise ValueError("unsupported split")
    if elements_y + 2 * reach > SLOTS or fields * width > 128 or width > ny:
        raise ValueError("unsupported block")
    lanes = -(-held * SLOTS // 128) * 128
    vmem, dma = pltpu.VMEM, pltpu.SemaphoreType.DMA
    f32 = jnp.float32
    anywhere = pl.BlockSpec(memory_space=pl.ANY)
    return pl.pallas_call(
        functools.partial(kernel, n, nz, nlev),
        out_shape=jax.ShapeDtypeStruct((nlev, tracers // nlev, nx, ny), f32),
        in_specs=[anywhere] * 4 + [pl.BlockSpec(memory_space=pltpu.SMEM)],
        out_specs=pl.BlockSpec(memory_space=pltpu.VMEM),
        scratch_shapes=[
            vmem((tracers, nx, ny), f32),
            vmem((3, nx, ny), f32),
            vmem((n, fields, nx, ny), f32),
            vmem((2, n, nx, 128), f32),
            vmem((fields, n * nx, ny), f32),
            vmem((2, n * nx, 128), f32),
            vmem((held * (ny + 128), GLL_NODES * lanes), jnp.bfloat16),
            vmem((GLL_NODES * lanes, held * ny), jnp.bfloat16),
            vmem((held, n * nx, ny), f32),
            vmem((nlev, tracers // nlev, nx, ny), f32),
            dma((4,)),
            dma((n,)),
            dma((n,)),
            dma((2, n)),
            dma((2, n)),
            dma((n,)),
            dma((nlev, n // nlev)),
        ],
        compiler_params=pltpu.CompilerParams(
            collective_id=0, has_side_effects=True, vmem_limit_bytes=32 * 1024 * 1024
        ),
        name="limited_step",
    )(tracer, node_mass, wind_x, wind_y, remap)


def solution(mesh):
    sizes = [mesh.shape[axis] for axis in ("px", "py", "lev")]
    in_specs = (
        P("lev", None, "px", "py"),
        P("lev", "px", "py"),
        P("lev", "px", "py"),
        P("lev", "px", "py"),
        P(),
    )
    out_specs = P(None, "lev", "px", "py")
    return jax.shard_map(
        functools.partial(shards, *sizes),
        mesh=mesh,
        in_specs=in_specs,
        out_specs=out_specs,
        check_vma=False,
    )
```

```python
import functools

import jax
import jax.numpy as jnp
import numpy as np
from jax import lax
from jax.experimental import pallas as pl
from jax.experimental.pallas import tpu as pltpu
from jax.sharding import PartitionSpec as P

GLL_NODES = 4
SECTION_REACH = 2
SLOTS = 64

sentinel = 1e30
step_size = 0.1
section_weights = ((0.0, 1.0), (0.75, 0.25), (1.0 / 3.0, 2.0 / 3.0))
MESH = pl.DeviceIdType.MESH


def derivative_table():
    points = np.array([-1.0, -(5.0 ** (-0.5)), 5.0 ** (-0.5), 1.0])
    number = points.shape[0]
    barycentric = np.array(
        [
            1.0
            / np.prod([points[outer] - points[inner] for inner in range(number) if inner != outer])
            for outer in range(number)
        ]
    )
    table = np.zeros((number, number))
    for outer in range(number):
        for inner in range(number):
            if inner != outer:
                table[outer, inner] = (
                    barycentric[inner] / barycentric[outer] / (points[outer] - points[inner])
                )
    for outer in range(number):
        table[outer, outer] = -np.sum(table[outer])
    return table


def rolled(values, shift, axis):
    size = values.shape[axis]
    shift %= size
    return pltpu.roll(values, shift, axis) if shift else values


def moved_by_table(values, table):
    rows = values.shape[0]
    high = values.astype(jnp.bfloat16)
    rest = values - high.astype(jnp.float32)
    middle = rest.astype(jnp.bfloat16)
    low = (rest - middle.astype(jnp.float32)).astype(jnp.bfloat16)
    terms = jnp.dot(
        jnp.concatenate([high, middle, low], axis=0), table, preferred_element_type=jnp.float32
    )
    return terms[:rows] + (terms[rows : 2 * rows] + terms[2 * rows :])


def sections(tracer, node_mass, wind_x, wind_y, inside):
    nodes = range(GLL_NODES)
    table = step_size * derivative_table()

    def node_sums(values):
        first = [values[0][j] + rolled(values[3][j], 1, 0) for j in nodes]
        last = [values[3][j] + rolled(values[0][j], -1, 0) for j in nodes]
        values = [first, values[1], values[2], last]
        return [
            [row[0] + rolled(row[3], 1, 1), row[1], row[2], row[3] + rolled(row[0], -1, 1)]
            for row in values
        ]

    def tree(combine, items):
        while len(items) > 1:
            items = [combine(*items[i : i + 2]) for i in range(0, len(items), 2)]
        return items[0]

    def around(combine, values):
        for axis in (0, 1):
            values = combine(
                combine(values, rolled(values, 1, axis)), rolled(values, -1, axis)
            )
        return values

    inverse = [
        [1.0 / jnp.where(inside, entry, 1.0) for entry in row] for row in node_sums(node_mass)
    ]
    field = tracer
    for share_start, share_new in section_weights:
        flat = [field[i][j] for i in nodes for j in nodes]
        lower = around(jnp.minimum, jnp.where(inside, tree(jnp.minimum, flat), sentinel))
        upper = around(jnp.maximum, jnp.where(inside, tree(jnp.maximum, flat), -sentinel))
        flux_x = [[wind_x[i][j] * field[i][j] for j in nodes] for i in nodes]
        flux_y = [[wind_y[i][j] * field[i][j] for j in nodes] for i in nodes]
        weighted = []
        for i in nodes:
            row = []
            for j in nodes:
                slope_x = tree(jnp.add, [float(table[i, k]) * flux_x[k][j] for k in nodes])
                slope_y = tree(jnp.add, [float(table[j, k]) * flux_y[i][k] for k in nodes])
                moved = field[i][j] - (slope_x + slope_y)
                limited = jnp.minimum(jnp.maximum(moved, lower), upper)
                row.append(node_mass[i][j] * limited)
            weighted.append(row)
        summed = node_sums(weighted)
        field = [
            [
                share_new * (summed[i][j] * inverse[i][j])
                + (share_start * tracer[i][j] if share_start else 0.0)
                for j in nodes
            ]
            for i in nodes
        ]
    return field


def kernel(
    n,
    nz,
    nlev,
    tracer_hbm,
    mass_hbm,
    wind_x_hbm,
    wind_y_hbm,
    remap_hbm,
    out,
    tracer_in,
    metric_in,
    remap,
    blocks_out,
    halos_out,
    blocks,
    halos,
    spread,
    gather,
    results_out,
    results,
    in_sem,
    block_send,
    block_recv,
    halo_send,
    halo_recv,
    result_send,
    result_recv,
):
    tracers, nx, ny = tracer_in.shape
    held = tracers // n
    fields = held + 3
    half = n // nlev
    reach = SECTION_REACH * len(section_weights)
    width = reach * GLL_NODES
    elements_y = ny // GLL_NODES
    elements_x = n * nx // GLL_NODES
    lanes = spread.shape[1] // GLL_NODES
    px, py, lev = lax.axis_index("px"), lax.axis_index("py"), lax.axis_index("lev")
    has_low, has_high = py > 0, py < nz - 1
    target_lev = px // half

    def others(number):
        return [lax.rem(px + d, n) for d in range(number)]

    barrier = pltpu.get_barrier_semaphore()

    def greet(x, y, level):
        pl.semaphore_signal(barrier, inc=1, device_id=(x, y, level), device_id_type=MESH)

    for d, x in enumerate(others(n)):
        pl.when(has_low)(functools.partial(greet, x, py - 1, lev))
        pl.when(has_high)(functools.partial(greet, x, py + 1, lev))
        for step in range(nlev):
            if d or step:
                greet(x, py, lax.rem(lev + step, nlev))

    copies = [pltpu.make_async_copy(tracer_hbm.at[0], tracer_in, in_sem.at[0])]
    for k, source in enumerate((mass_hbm, wind_x_hbm, wind_y_hbm)):
        copies.append(pltpu.make_async_copy(source.at[0], metric_in.at[k], in_sem.at[k + 1]))
    remap_copy = pltpu.make_async_copy(remap_hbm, remap, in_sem.at[4])
    remap_copy.start()
    for copy in copies:
        copy.start()
    for copy in copies:
        copy.wait()
    remap_copy.wait()

    lane = lax.broadcasted_iota(jnp.int32, (nx, halos.shape[2]), 1)

    def halo_tile(group, side):
        tile = jnp.zeros(lane.shape, jnp.float32)
        for k in range(fields):
            piece = tracer_in[group * held + k] if k < held else metric_in[k - held]
            shift = width * k - (ny - width if side else 0)
            wanted = (lane >= width * k) & (lane < width * (k + 1))
            tile = jnp.where(wanted, rolled(piece, shift, 1), tile)
        return tile

    for group in range(n):
        blocks_out[group, :held] = tracer_in[group * held : (group + 1) * held]
        blocks_out[group, held:] = metric_in[...]
        for side in range(2):
            halos_out[side, group] = halo_tile(group, side)

    peers = n * nlev - 1
    pl.semaphore_wait(
        barrier, peers + n * (has_low.astype(jnp.int32) + has_high.astype(jnp.int32))
    )

    mine = pl.ds(pl.multiple_of(px * nx, nx), nx)

    def block_copy(x):
        return pltpu.make_async_remote_copy(
            src_ref=blocks_out.at[x],
            dst_ref=blocks.at[:, mine, :],
            send_sem=block_send.at[x],
            recv_sem=block_recv.at[px],
            device_id=(x, py, lev),
            device_id_type=MESH,
        )

    def halo_copy(x, side):
        return pltpu.make_async_remote_copy(
            src_ref=halos_out.at[side, x],
            dst_ref=halos.at[side, mine, :],
            send_sem=halo_send.at[side, x],
            recv_sem=halo_recv.at[side, px],
            device_id=(x, py + (1 if side else -1), lev),
            device_id_type=MESH,
        )

    sides = ((0, has_low, has_high), (1, has_high, has_low))
    for x in others(n)[1:]:
        block_copy(x).start()
    for side, sends, _ in sides:
        for x in others(n):

            @pl.when(sends)
            def _(side=side, x=x):
                halo_copy(x, side).start()

    blocks[:, mine, :] = blocks_out[px]
    for side, _, gets in sides:

        @pl.when(jnp.logical_not(gets))
        def _(side=side):
            halos[side] = jnp.zeros(halos.shape[1:], jnp.float32)

    def node_of(shape, axis):
        return lax.broadcasted_iota(jnp.int32, shape, axis)

    depth = ny + halos.shape[2]
    source = node_of((depth, 1), 0)
    slot = jnp.where(
        source < ny + width,
        reach + source // GLL_NODES,
        jnp.where(source < ny + 2 * width, (source - ny - width) // GLL_NODES, -SLOTS * lanes),
    )
    place = lax.rem(source, GLL_NODES) * lanes + slot
    column = node_of((1, spread.shape[1]), 1)
    for k in range(held):
        spread[k * depth : (k + 1) * depth] = jnp.where(
            place + k * SLOTS == column, 1.0, 0.0
        ).astype(jnp.bfloat16)
    source = node_of((gather.shape[0], 1), 0)
    at = lax.rem(source, lanes)
    element = lax.rem(at, SLOTS) - reach
    kept = (element >= 0) & (element < elements_y) & (at // SLOTS < held)
    place = jnp.where(
        kept, at // SLOTS * ny + element * GLL_NODES + source // lanes, -1
    )
    gather[...] = jnp.where(place == node_of((1, gather.shape[1]), 1), 1.0, 0.0).astype(
        jnp.bfloat16
    )

    for x in others(n)[1:]:
        rows = pl.ds(pl.multiple_of(x * nx, nx), nx)
        pltpu.make_async_remote_copy(
            src_ref=blocks_out.at[x],
            dst_ref=blocks.at[:, rows, :],
            send_sem=block_send.at[x],
            recv_sem=block_recv.at[x],
            device_id=(x, py, lev),
            device_id_type=MESH,
        ).wait_recv()
    for side, _, gets in sides:
        for x in others(n):

            @pl.when(gets)
            def _(side=side, x=x):
                rows = pl.ds(pl.multiple_of(x * nx, nx), nx)
                pltpu.make_async_remote_copy(
                    src_ref=halos_out.at[side, x],
                    dst_ref=halos.at[side, rows, :],
                    send_sem=halo_send.at[side, x],
                    recv_sem=halo_recv.at[side, x],
                    device_id=(x, py + (-1 if side else 1), lev),
                    device_id_type=MESH,
                ).wait_recv()

    lane = lax.broadcasted_iota(jnp.int32, (elements_x, halos.shape[2]), 1)

    def operand(k):
        parts = []
        for i in range(GLL_NODES):
            rows = pl.ds(i, elements_x, stride=GLL_NODES)
            high = rolled(halos[0, rows, :], -width * k, 1)
            low = rolled(halos[1, rows, :], width - width * k, 1)
            halo = jnp.where(lane < width, high, jnp.where(lane < 2 * width, low, 0.0))
            parts.append(jnp.concatenate([blocks[k, rows, :], halo], axis=1))
        return jnp.concatenate(parts, axis=0)

    def by_node(values):
        return [
            [
                values[i * elements_x : (i + 1) * elements_x, j * lanes : (j + 1) * lanes]
                for j in range(GLL_NODES)
            ]
            for i in range(GLL_NODES)
        ]

    tracer = by_node(
        moved_by_table(jnp.concatenate([operand(k) for k in range(held)], axis=1), spread[...])
    )
    everywhere = spread[:depth]
    for k in range(1, held):
        everywhere = everywhere + spread[k * depth : (k + 1) * depth]
    metric = moved_by_table(
        jnp.concatenate([operand(held + k) for k in range(3)], axis=0), everywhere
    )
    rows = GLL_NODES * elements_x
    node_mass, wind_x, wind_y = (by_node(metric[k * rows : (k + 1) * rows]) for k in range(3))

    slot = lax.rem(lax.broadcasted_iota(jnp.int32, (elements_x, lanes), 1), SLOTS)
    element = py * elements_y + slot - reach
    inside = (slot < elements_y + 2 * reach) & (element >= 0) & (element < nz * elements_y)
    evolved = sections(tracer, node_mass, wind_x, wind_y, inside)

    evolved = moved_by_table(
        jnp.concatenate([jnp.concatenate(row, axis=1) for row in evolved], axis=0), gather[...]
    )
    for k in range(held):
        for i in range(GLL_NODES):
            results_out[k, pl.ds(i, elements_x, stride=GLL_NODES), :] = evolved[
                i * elements_x : (i + 1) * elements_x, k * ny : (k + 1) * ny
            ]

    def result_copy(x, level, holder, to):
        return pltpu.make_async_remote_copy(
            src_ref=results_out.at[:, pl.ds(pl.multiple_of(x * nx, nx), nx), :],
            dst_ref=results.at[level, pl.ds(holder * held, held)],
            send_sem=result_send.at[x],
            recv_sem=result_recv.at[level, holder],
            device_id=to,
            device_id_type=MESH,
        )

    holder = lax.rem(px, half)
    for d, x in enumerate(others(n)):
        copy = result_copy(x, lev, holder, (x, py, target_lev))
        if d:
            copy.start()
        else:
            pl.when(target_lev != lev)(copy.start)

    @pl.when(target_lev == lev)
    def _():
        results[lev, pl.ds(holder * held, held)] = results_out[:, mine, :]

    for level in range(nlev):
        for j in range(half):
            x = lev * half + j

            @pl.when(jnp.logical_or(x != px, lev != level))
            def _(x=x, level=level, j=j):
                result_copy(px, level, j, (x, py, level)).wait_recv()

    for a in range(nlev):
        total = remap[a, 0] * results[0]
        for b in range(1, nlev):
            total = total + remap[a, b] * results[b]
        out[a] = total

    for x in others(n)[1:]:
        block_copy(x).wait_send()
    for side, sends, _ in sides:
        for x in others(n):

            @pl.when(sends)
            def _(side=side, x=x):
                halo_copy(x, side).wait_send()

    for d, x in enumerate(others(n)):
        copy = result_copy(x, lev, holder, (x, py, target_lev))
        if d:
            copy.wait_send()
        else:
            pl.when(target_lev != lev)(copy.wait_send)


def shards(n, nz, nlev, tracer, node_mass, wind_x, wind_y, remap):
    levels, tracers, nx, ny = tracer.shape
    held = tracers // n
    fields = held + 3
    reach = SECTION_REACH * len(section_weights)
    width = reach * GLL_NODES
    elements_y = ny // GLL_NODES
    if levels != 1 or tracers % n or n % nlev or nx % 8 or ny % 128:
        raise ValueError("unsupported split")
    if elements_y + 2 * reach > SLOTS or fields * width > 128 or width > ny:
        raise ValueError("unsupported block")
    lanes = -(-held * SLOTS // 128) * 128
    vmem, dma = pltpu.VMEM, pltpu.SemaphoreType.DMA
    f32 = jnp.float32
    anywhere = pl.BlockSpec(memory_space=pltpu.HBM)
    return pl.pallas_call(
        functools.partial(kernel, n, nz, nlev),
        out_shape=jax.ShapeDtypeStruct((nlev, tracers // nlev, nx, ny), f32),
        in_specs=[anywhere] * 5,
        out_specs=pl.BlockSpec(memory_space=pltpu.VMEM),
        scratch_shapes=[
            vmem((tracers, nx, ny), f32),
            vmem((3, nx, ny), f32),
            pltpu.SMEM(remap.shape, f32),
            vmem((n, fields, nx, ny), f32),
            vmem((2, n, nx, 128), f32),
            vmem((fields, n * nx, ny), f32),
            vmem((2, n * nx, 128), f32),
            vmem((held * (ny + 128), GLL_NODES * lanes), jnp.bfloat16),
            vmem((GLL_NODES * lanes, held * ny), jnp.bfloat16),
            vmem((held, n * nx, ny), f32),
            vmem((nlev, tracers // nlev, nx, ny), f32),
            dma((5,)),
            dma((n,)),
            dma((n,)),
            dma((2, n)),
            dma((2, n)),
            dma((n,)),
            dma((nlev, n // nlev)),
        ],
        compiler_params=pltpu.CompilerParams(
            collective_id=0, has_side_effects=True, vmem_limit_bytes=60 * 1024 * 1024
        ),
        name="limited_step",
    )(tracer, node_mass, wind_x, wind_y, remap)


def solution(mesh):
    sizes = [mesh.shape[axis] for axis in ("px", "py", "lev")]
    in_specs = (
        P("lev", None, "px", "py"),
        P("lev", "px", "py"),
        P("lev", "px", "py"),
        P("lev", "px", "py"),
        P(),
    )
    out_specs = P(None, "lev", "px", "py")
    return jax.shard_map(
        functools.partial(shards, *sizes),
        mesh=mesh,
        in_specs=in_specs,
        out_specs=out_specs,
        check_vma=False,
    )
```

```python
import functools

import jax
import jax.numpy as jnp
import numpy as np
from jax import lax
from jax.experimental import pallas as pl
from jax.experimental.pallas import tpu as pltpu
from jax.sharding import PartitionSpec as P

GLL_NODES = 4
SECTION_REACH = 2
SLOTS = 64

sentinel = 1e30
step_size = 0.1
section_weights = ((0.0, 1.0), (0.75, 0.25), (1.0 / 3.0, 2.0 / 3.0))
MESH = pl.DeviceIdType.MESH


def derivative_table():
    points = np.array([-1.0, -(5.0 ** (-0.5)), 5.0 ** (-0.5), 1.0])
    number = points.shape[0]
    barycentric = np.array(
        [
            1.0
            / np.prod([points[outer] - points[inner] for inner in range(number) if inner != outer])
            for outer in range(number)
        ]
    )
    table = np.zeros((number, number))
    for outer in range(number):
        for inner in range(number):
            if inner != outer:
                table[outer, inner] = (
                    barycentric[inner] / barycentric[outer] / (points[outer] - points[inner])
                )
    for outer in range(number):
        table[outer, outer] = -np.sum(table[outer])
    return table


def rolled(values, shift, axis):
    size = values.shape[axis]
    shift %= size
    return pltpu.roll(values, shift, axis) if shift else values


def moved_by_table(values, table):
    rows = values.shape[0]
    high = values.astype(jnp.bfloat16)
    rest = values - high.astype(jnp.float32)
    middle = rest.astype(jnp.bfloat16)
    low = (rest - middle.astype(jnp.float32)).astype(jnp.bfloat16)
    terms = jnp.dot(
        jnp.concatenate([high, middle, low], axis=0), table, preferred_element_type=jnp.float32
    )
    return terms[:rows] + (terms[rows : 2 * rows] + terms[2 * rows :])


def sections(tracer, node_mass, wind_x, wind_y, inside):
    nodes = range(GLL_NODES)
    table = step_size * derivative_table()

    def node_sums(values):
        first = [values[0][j] + rolled(values[3][j], 1, 0) for j in nodes]
        last = [values[3][j] + rolled(values[0][j], -1, 0) for j in nodes]
        values = [first, values[1], values[2], last]
        return [
            [row[0] + rolled(row[3], 1, 1), row[1], row[2], row[3] + rolled(row[0], -1, 1)]
            for row in values
        ]

    def tree(combine, items):
        while len(items) > 1:
            items = [combine(*items[i : i + 2]) for i in range(0, len(items), 2)]
        return items[0]

    def around(combine, values):
        for axis in (0, 1):
            values = combine(
                combine(values, rolled(values, 1, axis)), rolled(values, -1, axis)
            )
        return values

    inverse = [
        [1.0 / jnp.where(inside, entry, 1.0) for entry in row] for row in node_sums(node_mass)
    ]
    field = tracer
    for share_start, share_new in section_weights:
        flat = [field[i][j] for i in nodes for j in nodes]
        lower = around(jnp.minimum, jnp.where(inside, tree(jnp.minimum, flat), sentinel))
        upper = around(jnp.maximum, jnp.where(inside, tree(jnp.maximum, flat), -sentinel))
        flux_x = [[wind_x[i][j] * field[i][j] for j in nodes] for i in nodes]
        flux_y = [[wind_y[i][j] * field[i][j] for j in nodes] for i in nodes]
        weighted = []
        for i in nodes:
            row = []
            for j in nodes:
                slope_x = tree(jnp.add, [float(table[i, k]) * flux_x[k][j] for k in nodes])
                slope_y = tree(jnp.add, [float(table[j, k]) * flux_y[i][k] for k in nodes])
                moved = field[i][j] - (slope_x + slope_y)
                limited = jnp.minimum(jnp.maximum(moved, lower), upper)
                row.append(node_mass[i][j] * limited)
            weighted.append(row)
        summed = node_sums(weighted)
        field = [
            [
                share_new * (summed[i][j] * inverse[i][j])
                + (share_start * tracer[i][j] if share_start else 0.0)
                for j in nodes
            ]
            for i in nodes
        ]
    return field


def kernel(
    n,
    nz,
    nlev,
    tracer_hbm,
    mass_hbm,
    wind_x_hbm,
    wind_y_hbm,
    remap_hbm,
    out,
    tracer_in,
    metric_in,
    remap,
    blocks_out,
    halos_out,
    blocks,
    halos,
    spread,
    gather,
    results_out,
    results,
    in_sem,
    block_send,
    block_recv,
    halo_send,
    halo_recv,
    result_send,
    result_recv,
):
    tracers, nx, ny = tracer_in.shape
    held = tracers // n
    fields = held + 3
    half = n // nlev
    reach = SECTION_REACH * len(section_weights)
    width = reach * GLL_NODES
    elements_y = ny // GLL_NODES
    elements_x = n * nx // GLL_NODES
    lanes = spread.shape[1] // GLL_NODES
    px, py, lev = lax.axis_index("px"), lax.axis_index("py"), lax.axis_index("lev")
    has_low, has_high = py > 0, py < nz - 1
    target_lev = px // half

    def others(number):
        return [lax.rem(px + d, n) for d in range(number)]

    barrier = pltpu.get_barrier_semaphore()

    def greet(x, y, level):
        pl.semaphore_signal(barrier, inc=1, device_id=(x, y, level), device_id_type=MESH)

    for d, x in enumerate(others(n)):
        pl.when(has_low)(functools.partial(greet, x, py - 1, lev))
        pl.when(has_high)(functools.partial(greet, x, py + 1, lev))
        for step in range(nlev):
            if d or step:
                greet(x, py, lax.rem(lev + step, nlev))

    copies = [pltpu.make_async_copy(tracer_hbm.at[0], tracer_in, in_sem.at[0])]
    for k, source in enumerate((mass_hbm, wind_x_hbm, wind_y_hbm)):
        copies.append(pltpu.make_async_copy(source.at[0], metric_in.at[k], in_sem.at[k + 1]))
    remap_copy = pltpu.make_async_copy(remap_hbm, remap, in_sem.at[4])
    remap_copy.start()
    for copy in copies:
        copy.start()
    for copy in copies:
        copy.wait()


    lane = lax.broadcasted_iota(jnp.int32, (nx, halos.shape[2]), 1)

    def halo_tile(group, side):
        tile = jnp.zeros(lane.shape, jnp.float32)
        for k in range(fields):
            piece = tracer_in[group * held + k] if k < held else metric_in[k - held]
            shift = width * k - (ny - width if side else 0)
            wanted = (lane >= width * k) & (lane < width * (k + 1))
            tile = jnp.where(wanted, rolled(piece, shift, 1), tile)
        return tile

    for group in range(n):
        blocks_out[group, :held] = tracer_in[group * held : (group + 1) * held]
        blocks_out[group, held:] = metric_in[...]
        for side in range(2):
            halos_out[side, group] = halo_tile(group, side)

    peers = n * nlev - 1
    pl.semaphore_wait(
        barrier, peers + n * (has_low.astype(jnp.int32) + has_high.astype(jnp.int32))
    )

    mine = pl.ds(pl.multiple_of(px * nx, nx), nx)

    def block_copy(x):
        return pltpu.make_async_remote_copy(
            src_ref=blocks_out.at[x],
            dst_ref=blocks.at[:, mine, :],
            send_sem=block_send.at[x],
            recv_sem=block_recv.at[px],
            device_id=(x, py, lev),
            device_id_type=MESH,
        )

    def halo_copy(x, side):
        return pltpu.make_async_remote_copy(
            src_ref=halos_out.at[side, x],
            dst_ref=halos.at[side, mine, :],
            send_sem=halo_send.at[side, x],
            recv_sem=halo_recv.at[side, px],
            device_id=(x, py + (1 if side else -1), lev),
            device_id_type=MESH,
        )

    sides = ((0, has_low, has_high), (1, has_high, has_low))
    for x in others(n)[1:]:
        block_copy(x).start()
    for side, sends, _ in sides:
        for x in others(n):

            @pl.when(sends)
            def _(side=side, x=x):
                halo_copy(x, side).start()

    blocks[:, mine, :] = blocks_out[px]
    for side, _, gets in sides:

        @pl.when(jnp.logical_not(gets))
        def _(side=side):
            halos[side] = jnp.zeros(halos.shape[1:], jnp.float32)

    def node_of(shape, axis):
        return lax.broadcasted_iota(jnp.int32, shape, axis)

    depth = ny + halos.shape[2]
    source = node_of((depth, 1), 0)
    slot = jnp.where(
        source < ny + width,
        reach + source // GLL_NODES,
        jnp.where(source < ny + 2 * width, (source - ny - width) // GLL_NODES, -SLOTS * lanes),
    )
    place = lax.rem(source, GLL_NODES) * lanes + slot
    column = node_of((1, spread.shape[1]), 1)
    for k in range(held):
        spread[k * depth : (k + 1) * depth] = jnp.where(
            place + k * SLOTS == column, 1.0, 0.0
        ).astype(jnp.bfloat16)
    source = node_of((gather.shape[0], 1), 0)
    at = lax.rem(source, lanes)
    element = lax.rem(at, SLOTS) - reach
    kept = (element >= 0) & (element < elements_y) & (at // SLOTS < held)
    place = jnp.where(
        kept, at // SLOTS * ny + element * GLL_NODES + source // lanes, -1
    )
    gather[...] = jnp.where(place == node_of((1, gather.shape[1]), 1), 1.0, 0.0).astype(
        jnp.bfloat16
    )

    for x in others(n)[1:]:
        rows = pl.ds(pl.multiple_of(x * nx, nx), nx)
        pltpu.make_async_remote_copy(
            src_ref=blocks_out.at[x],
            dst_ref=blocks.at[:, rows, :],
            send_sem=block_send.at[x],
            recv_sem=block_recv.at[x],
            device_id=(x, py, lev),
            device_id_type=MESH,
        ).wait_recv()
    for side, _, gets in sides:
        for x in others(n):

            @pl.when(gets)
            def _(side=side, x=x):
                rows = pl.ds(pl.multiple_of(x * nx, nx), nx)
                pltpu.make_async_remote_copy(
                    src_ref=halos_out.at[side, x],
                    dst_ref=halos.at[side, rows, :],
                    send_sem=halo_send.at[side, x],
                    recv_sem=halo_recv.at[side, x],
                    device_id=(x, py + (-1 if side else 1), lev),
                    device_id_type=MESH,
                ).wait_recv()

    lane = lax.broadcasted_iota(jnp.int32, (elements_x, halos.shape[2]), 1)

    def operand(k):
        parts = []
        for i in range(GLL_NODES):
            rows = pl.ds(i, elements_x, stride=GLL_NODES)
            high = rolled(halos[0, rows, :], -width * k, 1)
            low = rolled(halos[1, rows, :], width - width * k, 1)
            halo = jnp.where(lane < width, high, jnp.where(lane < 2 * width, low, 0.0))
            parts.append(jnp.concatenate([blocks[k, rows, :], halo], axis=1))
        return jnp.concatenate(parts, axis=0)

    def by_node(values):
        return [
            [
                values[i * elements_x : (i + 1) * elements_x, j * lanes : (j + 1) * lanes]
                for j in range(GLL_NODES)
            ]
            for i in range(GLL_NODES)
        ]

    tracer = by_node(
        moved_by_table(jnp.concatenate([operand(k) for k in range(held)], axis=1), spread[...])
    )
    everywhere = spread[:depth]
    for k in range(1, held):
        everywhere = everywhere + spread[k * depth : (k + 1) * depth]
    metric = moved_by_table(
        jnp.concatenate([operand(held + k) for k in range(3)], axis=0), everywhere
    )
    rows = GLL_NODES * elements_x
    node_mass, wind_x, wind_y = (by_node(metric[k * rows : (k + 1) * rows]) for k in range(3))

    slot = lax.rem(lax.broadcasted_iota(jnp.int32, (elements_x, lanes), 1), SLOTS)
    element = py * elements_y + slot - reach
    inside = (slot < elements_y + 2 * reach) & (element >= 0) & (element < nz * elements_y)
    evolved = sections(tracer, node_mass, wind_x, wind_y, inside)

    evolved = moved_by_table(
        jnp.concatenate([jnp.concatenate(row, axis=1) for row in evolved], axis=0), gather[...]
    )
    for k in range(held):
        for i in range(GLL_NODES):
            results_out[k, pl.ds(i, elements_x, stride=GLL_NODES), :] = evolved[
                i * elements_x : (i + 1) * elements_x, k * ny : (k + 1) * ny
            ]

    def result_copy(x, level, holder, to):
        return pltpu.make_async_remote_copy(
            src_ref=results_out.at[:, pl.ds(pl.multiple_of(x * nx, nx), nx), :],
            dst_ref=results.at[level, pl.ds(holder * held, held)],
            send_sem=result_send.at[x],
            recv_sem=result_recv.at[level, holder],
            device_id=to,
            device_id_type=MESH,
        )

    holder = lax.rem(px, half)
    for d, x in enumerate(others(n)):
        copy = result_copy(x, lev, holder, (x, py, target_lev))
        if d:
            copy.start()
        else:
            pl.when(target_lev != lev)(copy.start)

    @pl.when(target_lev == lev)
    def _():
        results[lev, pl.ds(holder * held, held)] = results_out[:, mine, :]

    for level in range(nlev):
        for j in range(half):
            x = lev * half + j

            @pl.when(jnp.logical_or(x != px, lev != level))
            def _(x=x, level=level, j=j):
                result_copy(px, level, j, (x, py, level)).wait_recv()

    remap_copy.wait()
    for a in range(nlev):
        total = remap[a, 0] * results[0]
        for b in range(1, nlev):
            total = total + remap[a, b] * results[b]
        out[a] = total

    for x in others(n)[1:]:
        block_copy(x).wait_send()
    for side, sends, _ in sides:
        for x in others(n):

            @pl.when(sends)
            def _(side=side, x=x):
                halo_copy(x, side).wait_send()

    for d, x in enumerate(others(n)):
        copy = result_copy(x, lev, holder, (x, py, target_lev))
        if d:
            copy.wait_send()
        else:
            pl.when(target_lev != lev)(copy.wait_send)


def shards(n, nz, nlev, tracer, node_mass, wind_x, wind_y, remap):
    levels, tracers, nx, ny = tracer.shape
    held = tracers // n
    fields = held + 3
    reach = SECTION_REACH * len(section_weights)
    width = reach * GLL_NODES
    elements_y = ny // GLL_NODES
    if levels != 1 or tracers % n or n % nlev or nx % 8 or ny % 128:
        raise ValueError("unsupported split")
    if elements_y + 2 * reach > SLOTS or fields * width > 128 or width > ny:
        raise ValueError("unsupported block")
    lanes = -(-held * SLOTS // 128) * 128
    vmem, dma = pltpu.VMEM, pltpu.SemaphoreType.DMA
    f32 = jnp.float32
    anywhere = pl.BlockSpec(memory_space=pltpu.HBM)
    return pl.pallas_call(
        functools.partial(kernel, n, nz, nlev),
        out_shape=vmem((nlev, tracers // nlev, nx, ny), f32),
        in_specs=[anywhere] * 5,
        out_specs=pl.BlockSpec(memory_space=pltpu.VMEM),
        scratch_shapes=[
            vmem((tracers, nx, ny), f32),
            vmem((3, nx, ny), f32),
            pltpu.SMEM(remap.shape, f32),
            vmem((n, fields, nx, ny), f32),
            vmem((2, n, nx, 128), f32),
            vmem((fields, n * nx, ny), f32),
            vmem((2, n * nx, 128), f32),
            vmem((held * (ny + 128), GLL_NODES * lanes), jnp.bfloat16),
            vmem((GLL_NODES * lanes, held * ny), jnp.bfloat16),
            vmem((held, n * nx, ny), f32),
            vmem((nlev, tracers // nlev, nx, ny), f32),
            dma((5,)),
            dma((n,)),
            dma((n,)),
            dma((2, n)),
            dma((2, n)),
            dma((n,)),
            dma((nlev, n // nlev)),
        ],
        compiler_params=pltpu.CompilerParams(
            collective_id=0, has_side_effects=True, vmem_limit_bytes=32 * 1024 * 1024
        ),
        name="limited_step",
    )(
        *(
            pltpu.with_memory_space_constraint(operand, pltpu.HBM)
            for operand in (tracer, node_mass, wind_x, wind_y, remap)
        )
    )


def solution(mesh):
    sizes = [mesh.shape[axis] for axis in ("px", "py", "lev")]
    in_specs = (
        P("lev", None, "px", "py"),
        P("lev", "px", "py"),
        P("lev", "px", "py"),
        P("lev", "px", "py"),
        P(),
    )
    out_specs = P(None, "lev", "px", "py")
    return jax.shard_map(
        functools.partial(shards, *sizes),
        mesh=mesh,
        in_specs=in_specs,
        out_specs=out_specs,
        check_vma=False,
    )
```

```python
import functools

import jax
import jax.numpy as jnp
import numpy as np
from jax import lax
from jax.experimental import pallas as pl
from jax.experimental.pallas import tpu as pltpu
from jax.sharding import PartitionSpec as P

GLL_NODES = 4
SECTION_REACH = 2
SLOTS = 64

sentinel = 1e30
step_size = 0.1
section_weights = ((0.0, 1.0), (0.75, 0.25), (1.0 / 3.0, 2.0 / 3.0))
MESH = pl.DeviceIdType.MESH


def derivative_table():
    points = np.array([-1.0, -(5.0 ** (-0.5)), 5.0 ** (-0.5), 1.0])
    number = points.shape[0]
    barycentric = np.array(
        [
            1.0
            / np.prod([points[outer] - points[inner] for inner in range(number) if inner != outer])
            for outer in range(number)
        ]
    )
    table = np.zeros((number, number))
    for outer in range(number):
        for inner in range(number):
            if inner != outer:
                table[outer, inner] = (
                    barycentric[inner] / barycentric[outer] / (points[outer] - points[inner])
                )
    for outer in range(number):
        table[outer, outer] = -np.sum(table[outer])
    return table


def rolled(values, shift, axis):
    size = values.shape[axis]
    shift %= size
    return pltpu.roll(values, shift, axis) if shift else values


def moved_by_table(values, table):
    rows = values.shape[0]
    high = values.astype(jnp.bfloat16)
    low = (values - high.astype(jnp.float32)).astype(jnp.bfloat16)
    terms = jnp.dot(
        jnp.concatenate([high, low], axis=0), table, preferred_element_type=jnp.float32
    )
    return terms[:rows] + terms[rows:]


def sections(tracer, node_mass, wind_x, wind_y, inside):
    nodes = range(GLL_NODES)
    table = step_size * derivative_table()

    def node_sums(values):
        first = [values[0][j] + rolled(values[3][j], 1, 0) for j in nodes]
        last = [values[3][j] + rolled(values[0][j], -1, 0) for j in nodes]
        values = [first, values[1], values[2], last]
        return [
            [row[0] + rolled(row[3], 1, 1), row[1], row[2], row[3] + rolled(row[0], -1, 1)]
            for row in values
        ]

    def tree(combine, items):
        while len(items) > 1:
            items = [combine(*items[i : i + 2]) for i in range(0, len(items), 2)]
        return items[0]

    def around(combine, values):
        for axis in (0, 1):
            values = combine(
                combine(values, rolled(values, 1, axis)), rolled(values, -1, axis)
            )
        return values

    inverse = [
        [1.0 / jnp.where(inside, entry, 1.0) for entry in row] for row in node_sums(node_mass)
    ]
    field = tracer
    for share_start, share_new in section_weights:
        flat = [field[i][j] for i in nodes for j in nodes]
        lower = around(jnp.minimum, jnp.where(inside, tree(jnp.minimum, flat), sentinel))
        upper = around(jnp.maximum, jnp.where(inside, tree(jnp.maximum, flat), -sentinel))
        flux_x = [[wind_x[i][j] * field[i][j] for j in nodes] for i in nodes]
        flux_y = [[wind_y[i][j] * field[i][j] for j in nodes] for i in nodes]
        weighted = []
        for i in nodes:
            row = []
            for j in nodes:
                slope_x = tree(jnp.add, [float(table[i, k]) * flux_x[k][j] for k in nodes])
                slope_y = tree(jnp.add, [float(table[j, k]) * flux_y[i][k] for k in nodes])
                moved = field[i][j] - (slope_x + slope_y)
                limited = jnp.minimum(jnp.maximum(moved, lower), upper)
                row.append(node_mass[i][j] * limited)
            weighted.append(row)
        summed = node_sums(weighted)
        field = [
            [
                share_new * (summed[i][j] * inverse[i][j])
                + (share_start * tracer[i][j] if share_start else 0.0)
                for j in nodes
            ]
            for i in nodes
        ]
    return field


def kernel(
    n,
    nz,
    nlev,
    tracer_hbm,
    mass_hbm,
    wind_x_hbm,
    wind_y_hbm,
    remap_hbm,
    out,
    tracer_in,
    metric_in,
    remap,
    blocks_out,
    halos_out,
    blocks,
    halos,
    spread,
    gather,
    results_out,
    results,
    in_sem,
    block_send,
    block_recv,
    halo_send,
    halo_recv,
    result_send,
    result_recv,
):
    tracers, nx, ny = tracer_in.shape
    held = tracers // n
    fields = held + 3
    half = n // nlev
    reach = SECTION_REACH * len(section_weights)
    width = reach * GLL_NODES
    elements_y = ny // GLL_NODES
    elements_x = n * nx // GLL_NODES
    lanes = gather.shape[0] // GLL_NODES
    px, py, lev = lax.axis_index("px"), lax.axis_index("py"), lax.axis_index("lev")
    has_low, has_high = py > 0, py < nz - 1
    target_lev = px // half

    def others(number):
        return [lax.rem(px + d, n) for d in range(number)]

    copies = [pltpu.make_async_copy(tracer_hbm.at[0], tracer_in, in_sem.at[0])]
    for k, source in enumerate((mass_hbm, wind_x_hbm, wind_y_hbm)):
        copies.append(pltpu.make_async_copy(source.at[0], metric_in.at[k], in_sem.at[k + 1]))
    remap_copy = pltpu.make_async_copy(remap_hbm, remap, in_sem.at[4])
    remap_copy.start()
    for copy in copies:
        copy.start()

    barrier = pltpu.get_barrier_semaphore()

    def greet(x, y, level):
        pl.semaphore_signal(barrier, inc=1, device_id=(x, y, level), device_id_type=MESH)

    for d, x in enumerate(others(n)):
        pl.when(has_low)(functools.partial(greet, x, py - 1, lev))
        pl.when(has_high)(functools.partial(greet, x, py + 1, lev))
        for step in range(nlev):
            if d or step:
                greet(x, py, lax.rem(lev + step, nlev))

    for copy in copies:
        copy.wait()


    lane = lax.broadcasted_iota(jnp.int32, (nx, halos.shape[2]), 1)

    def halo_tile(group, side):
        tile = jnp.zeros(lane.shape, jnp.float32)
        for k in range(fields):
            piece = tracer_in[group * held + k] if k < held else metric_in[k - held]
            shift = width * k - (ny - width if side else 0)
            wanted = (lane >= width * k) & (lane < width * (k + 1))
            tile = jnp.where(wanted, rolled(piece, shift, 1), tile)
        return tile

    for group in range(n):
        blocks_out[group, :held] = tracer_in[group * held : (group + 1) * held]
        blocks_out[group, held:] = metric_in[...]
        for side in range(2):
            halos_out[side, group] = halo_tile(group, side)

    peers = n * nlev - 1
    pl.semaphore_wait(
        barrier, peers + n * (has_low.astype(jnp.int32) + has_high.astype(jnp.int32))
    )

    mine = pl.ds(pl.multiple_of(px * nx, nx), nx)

    def block_copy(x):
        return pltpu.make_async_remote_copy(
            src_ref=blocks_out.at[x],
            dst_ref=blocks.at[:, mine, :],
            send_sem=block_send.at[x],
            recv_sem=block_recv.at[px],
            device_id=(x, py, lev),
            device_id_type=MESH,
        )

    def halo_copy(x, side):
        return pltpu.make_async_remote_copy(
            src_ref=halos_out.at[side, x],
            dst_ref=halos.at[side, mine, :],
            send_sem=halo_send.at[side, x],
            recv_sem=halo_recv.at[side, px],
            device_id=(x, py + (1 if side else -1), lev),
            device_id_type=MESH,
        )

    sides = ((0, has_low, has_high), (1, has_high, has_low))
    for side, sends, _ in sides:
        for x in others(n):

            @pl.when(sends)
            def _(side=side, x=x):
                halo_copy(x, side).start()
    for x in others(n)[1:]:
        block_copy(x).start()

    blocks[:, mine, :] = blocks_out[px]
    for side, _, gets in sides:

        @pl.when(jnp.logical_not(gets))
        def _(side=side):
            halos[side] = jnp.zeros(halos.shape[1:], jnp.float32)

    def node_of(shape, axis):
        return lax.broadcasted_iota(jnp.int32, shape, axis)

    depth = ny + halos.shape[2]
    source = node_of((depth, 1), 0)
    slot = jnp.where(
        source < ny + width,
        reach + source // GLL_NODES,
        jnp.where(source < ny + 2 * width, (source - ny - width) // GLL_NODES, -SLOTS * GLL_NODES),
    )
    place = lax.rem(source, GLL_NODES) * SLOTS + slot
    column = node_of((1, spread.shape[1]), 1)
    spread[...] = jnp.where(place == column, 1.0, 0.0).astype(jnp.bfloat16)
    source = node_of((gather.shape[0], 1), 0)
    at = lax.rem(source, lanes)
    element = lax.rem(at, SLOTS) - reach
    kept = (element >= 0) & (element < elements_y) & (at // SLOTS < held)
    place = jnp.where(
        kept, at // SLOTS * ny + element * GLL_NODES + source // lanes, -1
    )
    gather[...] = jnp.where(place == node_of((1, gather.shape[1]), 1), 1.0, 0.0).astype(
        jnp.bfloat16
    )

    for side, _, gets in sides:
        for x in others(n):

            @pl.when(gets)
            def _(side=side, x=x):
                rows = pl.ds(pl.multiple_of(x * nx, nx), nx)
                pltpu.make_async_remote_copy(
                    src_ref=halos_out.at[side, x],
                    dst_ref=halos.at[side, rows, :],
                    send_sem=halo_send.at[side, x],
                    recv_sem=halo_recv.at[side, x],
                    device_id=(x, py + (-1 if side else 1), lev),
                    device_id_type=MESH,
                ).wait_recv()

    lane = lax.broadcasted_iota(jnp.int32, (elements_x, halos.shape[2]), 1)
    rows_of = [pl.ds(i, elements_x, stride=GLL_NODES) for i in range(GLL_NODES)]
    rims = []
    for rows in rows_of:
        high, low = halos[0, rows, :], halos[1, rows, :]
        rims.append(
            [
                jnp.where(
                    lane < width,
                    rolled(high, -width * k, 1),
                    jnp.where(lane < 2 * width, rolled(low, width - width * k, 1), 0.0),
                )
                for k in range(fields)
            ]
        )

    for x in others(n)[1:]:
        rows = pl.ds(pl.multiple_of(x * nx, nx), nx)
        pltpu.make_async_remote_copy(
            src_ref=blocks_out.at[x],
            dst_ref=blocks.at[:, rows, :],
            send_sem=block_send.at[x],
            recv_sem=block_recv.at[x],
            device_id=(x, py, lev),
            device_id_type=MESH,
        ).wait_recv()

    parts = [
        jnp.concatenate([blocks[k, rows_of[i], :], rims[i][k]], axis=1)
        for k in range(fields)
        for i in range(GLL_NODES)
    ]
    spread_out = moved_by_table(jnp.concatenate(parts, axis=0), spread[...])
    pair = 2 * SLOTS
    in_first = lax.broadcasted_iota(jnp.int32, (elements_x, pair), 1) < SLOTS

    def joined(first, second, i, j):
        first, second = (
            spread_out[
                (k * GLL_NODES + i) * elements_x : (k * GLL_NODES + i + 1) * elements_x,
                j // 2 * pair : (j // 2 + 1) * pair,
            ]
            for k in (first, second)
        )
        if j % 2:
            first = rolled(first, SLOTS, 1)
        else:
            second = rolled(second, SLOTS, 1)
        return jnp.where(in_first, first, second)

    def by_node(pairs):
        return [
            [
                jnp.concatenate([joined(first, second, i, j) for first, second in pairs], axis=1)
                for j in range(GLL_NODES)
            ]
            for i in range(GLL_NODES)
        ]

    tracer = by_node([(k, min(k + 1, held - 1)) for k in range(0, held, 2)])
    node_mass, wind_x, wind_y = (
        by_node([(held + k, held + k)] * (lanes // pair)) for k in range(3)
    )

    slot = lax.rem(lax.broadcasted_iota(jnp.int32, (elements_x, lanes), 1), SLOTS)
    element = py * elements_y + slot - reach
    inside = (slot < elements_y + 2 * reach) & (element >= 0) & (element < nz * elements_y)
    evolved = sections(tracer, node_mass, wind_x, wind_y, inside)

    evolved = moved_by_table(
        jnp.concatenate([jnp.concatenate(row, axis=1) for row in evolved], axis=0), gather[...]
    )
    for k in range(held):
        for i in range(GLL_NODES):
            results_out[k, pl.ds(i, elements_x, stride=GLL_NODES), :] = evolved[
                i * elements_x : (i + 1) * elements_x, k * ny : (k + 1) * ny
            ]

    def result_copy(x, level, holder, to):
        return pltpu.make_async_remote_copy(
            src_ref=results_out.at[:, pl.ds(pl.multiple_of(x * nx, nx), nx), :],
            dst_ref=results.at[level, pl.ds(holder * held, held)],
            send_sem=result_send.at[x],
            recv_sem=result_recv.at[level, holder],
            device_id=to,
            device_id_type=MESH,
        )

    holder = lax.rem(px, half)
    for d, x in enumerate(others(n)):
        copy = result_copy(x, lev, holder, (x, py, target_lev))
        if d:
            copy.start()
        else:
            pl.when(target_lev != lev)(copy.start)

    @pl.when(target_lev == lev)
    def _():
        results[lev, pl.ds(holder * held, held)] = results_out[:, mine, :]

    for level in range(nlev):
        for j in range(half):
            x = lev * half + j

            @pl.when(jnp.logical_or(x != px, lev != level))
            def _(x=x, level=level, j=j):
                result_copy(px, level, j, (x, py, level)).wait_recv()

    remap_copy.wait()
    for a in range(nlev):
        total = remap[a, 0] * results[0]
        for b in range(1, nlev):
            total = total + remap[a, b] * results[b]
        out[a] = total

    for x in others(n)[1:]:
        block_copy(x).wait_send()
    for side, sends, _ in sides:
        for x in others(n):

            @pl.when(sends)
            def _(side=side, x=x):
                halo_copy(x, side).wait_send()

    for d, x in enumerate(others(n)):
        copy = result_copy(x, lev, holder, (x, py, target_lev))
        if d:
            copy.wait_send()
        else:
            pl.when(target_lev != lev)(copy.wait_send)


def shards(n, nz, nlev, tracer, node_mass, wind_x, wind_y, remap):
    levels, tracers, nx, ny = tracer.shape
    held = tracers // n
    fields = held + 3
    reach = SECTION_REACH * len(section_weights)
    width = reach * GLL_NODES
    elements_y = ny // GLL_NODES
    if levels != 1 or tracers % n or n % nlev or nx % 8 or ny % 128:
        raise ValueError("unsupported split")
    if elements_y + 2 * reach > SLOTS or fields * width > 128 or width > ny:
        raise ValueError("unsupported block")
    lanes = -(-held * SLOTS // 128) * 128
    vmem, dma = pltpu.VMEM, pltpu.SemaphoreType.DMA
    f32 = jnp.float32
    anywhere = pl.BlockSpec(memory_space=pltpu.HBM)
    return pl.pallas_call(
        functools.partial(kernel, n, nz, nlev),
        out_shape=vmem((nlev, tracers // nlev, nx, ny), f32),
        in_specs=[anywhere] * 5,
        out_specs=pl.BlockSpec(memory_space=pltpu.VMEM),
        scratch_shapes=[
            vmem((tracers, nx, ny), f32),
            vmem((3, nx, ny), f32),
            pltpu.SMEM(remap.shape, f32),
            vmem((n, fields, nx, ny), f32),
            vmem((2, n, nx, 128), f32),
            vmem((fields, n * nx, ny), f32),
            vmem((2, n * nx, 128), f32),
            vmem((ny + 128, GLL_NODES * SLOTS), jnp.bfloat16),
            vmem((GLL_NODES * lanes, held * ny), jnp.bfloat16),
            vmem((held, n * nx, ny), f32),
            vmem((nlev, tracers // nlev, nx, ny), f32),
            dma((5,)),
            dma((n,)),
            dma((n,)),
            dma((2, n)),
            dma((2, n)),
            dma((n,)),
            dma((nlev, n // nlev)),
        ],
        compiler_params=pltpu.CompilerParams(
            collective_id=0, has_side_effects=True, vmem_limit_bytes=32 * 1024 * 1024
        ),
        name="limited_step",
    )(
        *(
            pltpu.with_memory_space_constraint(operand, pltpu.HBM)
            for operand in (tracer, node_mass, wind_x, wind_y, remap)
        )
    )


def solution(mesh):
    sizes = [mesh.shape[axis] for axis in ("px", "py", "lev")]
    in_specs = (
        P("lev", None, "px", "py"),
        P("lev", "px", "py"),
        P("lev", "px", "py"),
        P("lev", "px", "py"),
        P(),
    )
    out_specs = P(None, "lev", "px", "py")
    return jax.shard_map(
        functools.partial(shards, *sizes),
        mesh=mesh,
        in_specs=in_specs,
        out_specs=out_specs,
        check_vma=False,
    )
```

```python
import functools

import jax
import jax.numpy as jnp
import numpy as np
from jax import lax
from jax.experimental import pallas as pl
from jax.experimental.pallas import tpu as pltpu
from jax.sharding import PartitionSpec as P

GLL_NODES = 4
SECTION_REACH = 2
SLOTS = 64

sentinel = 1e30
step_size = 0.1
section_weights = ((0.0, 1.0), (0.75, 0.25), (1.0 / 3.0, 2.0 / 3.0))
MESH = pl.DeviceIdType.MESH


def derivative_table():
    points = np.array([-1.0, -(5.0 ** (-0.5)), 5.0 ** (-0.5), 1.0])
    number = points.shape[0]
    barycentric = np.array(
        [
            1.0
            / np.prod([points[outer] - points[inner] for inner in range(number) if inner != outer])
            for outer in range(number)
        ]
    )
    table = np.zeros((number, number))
    for outer in range(number):
        for inner in range(number):
            if inner != outer:
                table[outer, inner] = (
                    barycentric[inner] / barycentric[outer] / (points[outer] - points[inner])
                )
    for outer in range(number):
        table[outer, outer] = -np.sum(table[outer])
    return table


def rolled(values, shift, axis):
    size = values.shape[axis]
    shift %= size
    return pltpu.roll(values, shift, axis) if shift else values


def moved_by_table(values, table):
    rows = values.shape[0]
    high = values.astype(jnp.bfloat16)
    low = (values - high.astype(jnp.float32)).astype(jnp.bfloat16)
    terms = jnp.dot(
        jnp.concatenate([high, low], axis=0), table, preferred_element_type=jnp.float32
    )
    return terms[:rows] + terms[rows:]


def sections(tracer, node_mass, wind_x, wind_y, inside):
    nodes = range(GLL_NODES)
    table = step_size * derivative_table()

    def node_sums(values):
        first = [values[0][j] + rolled(values[3][j], 1, 0) for j in nodes]
        last = [values[3][j] + rolled(values[0][j], -1, 0) for j in nodes]
        values = [first, values[1], values[2], last]
        return [
            [row[0] + rolled(row[3], 1, 1), row[1], row[2], row[3] + rolled(row[0], -1, 1)]
            for row in values
        ]

    def tree(combine, items):
        while len(items) > 1:
            items = [combine(*items[i : i + 2]) for i in range(0, len(items), 2)]
        return items[0]

    def around(combine, values):
        for axis in (0, 1):
            values = combine(
                combine(values, rolled(values, 1, axis)), rolled(values, -1, axis)
            )
        return values

    inverse = [
        [1.0 / jnp.where(inside, entry, 1.0) for entry in row] for row in node_sums(node_mass)
    ]
    field = tracer
    for share_start, share_new in section_weights:
        flat = [field[i][j] for i in nodes for j in nodes]
        lower = around(jnp.minimum, jnp.where(inside, tree(jnp.minimum, flat), sentinel))
        upper = around(jnp.maximum, jnp.where(inside, tree(jnp.maximum, flat), -sentinel))
        flux_x = [[wind_x[i][j] * field[i][j] for j in nodes] for i in nodes]
        flux_y = [[wind_y[i][j] * field[i][j] for j in nodes] for i in nodes]
        weighted = []
        for i in nodes:
            row = []
            for j in nodes:
                slope_x = tree(jnp.add, [float(table[i, k]) * flux_x[k][j] for k in nodes])
                slope_y = tree(jnp.add, [float(table[j, k]) * flux_y[i][k] for k in nodes])
                moved = field[i][j] - (slope_x + slope_y)
                limited = jnp.minimum(jnp.maximum(moved, lower), upper)
                row.append(node_mass[i][j] * limited)
            weighted.append(row)
        summed = node_sums(weighted)
        field = [
            [
                share_new * (summed[i][j] * inverse[i][j])
                + (share_start * tracer[i][j] if share_start else 0.0)
                for j in nodes
            ]
            for i in nodes
        ]
    return field


def kernel(
    n,
    nz,
    nlev,
    tracer_hbm,
    mass_hbm,
    wind_x_hbm,
    wind_y_hbm,
    remap_hbm,
    out,
    tracer_in,
    metric_in,
    remap,
    blocks_out,
    halos_out,
    blocks,
    halos,
    spread,
    gather,
    results_out,
    results,
    in_sem,
    block_send,
    block_recv,
    halo_send,
    halo_recv,
    result_send,
    result_recv,
):
    tracers, nx, ny = tracer_in.shape
    held = tracers // n
    fields = held + 3
    half = n // nlev
    reach = SECTION_REACH * len(section_weights)
    width = reach * GLL_NODES
    elements_y = ny // GLL_NODES
    elements_x = n * nx // GLL_NODES
    lanes = gather.shape[0] // GLL_NODES
    px, py, lev = lax.axis_index("px"), lax.axis_index("py"), lax.axis_index("lev")
    has_low, has_high = py > 0, py < nz - 1
    target_lev = px // half

    def others():
        return [lax.rem(px + d, n) for d in sorted(range(1, n), key=lambda d: abs(2 * d - n))]

    everyone = others() + [px]

    def took(ref, sem):
        pltpu.make_async_copy(ref, ref, sem).wait()

    copies = [pltpu.make_async_copy(tracer_hbm.at[0], tracer_in, in_sem.at[0])]
    for k, source in enumerate((mass_hbm, wind_x_hbm, wind_y_hbm)):
        copies.append(pltpu.make_async_copy(source.at[0], metric_in.at[k], in_sem.at[k + 1]))
    remap_copy = pltpu.make_async_copy(remap_hbm, remap, in_sem.at[4])
    remap_copy.start()
    for copy in copies:
        copy.start()

    barrier = pltpu.get_barrier_semaphore()

    def greet(x, y, level):
        pl.semaphore_signal(barrier, inc=1, device_id=(x, y, level), device_id_type=MESH)

    for near, there in ((has_low, py - 1), (has_high, py + 1)):

        @pl.when(near)
        def _(there=there):
            for x in everyone:
                greet(x, there, lev)

    for x in everyone:
        for step in range(1, nlev):
            greet(x, py, lax.rem(lev + step, nlev))
    for x in others():
        greet(x, py, lev)

    for copy in copies:
        copy.wait()


    lane = lax.broadcasted_iota(jnp.int32, (nx, halos.shape[2]), 1)

    def halo_tile(group, side):
        tile = jnp.zeros(lane.shape, jnp.float32)
        for k in range(fields):
            piece = tracer_in[group * held + k] if k < held else metric_in[k - held]
            shift = width * k - (ny - width if side else 0)
            wanted = (lane >= width * k) & (lane < width * (k + 1))
            tile = jnp.where(wanted, rolled(piece, shift, 1), tile)
        return tile

    for group in range(n):
        blocks_out[group, :held] = tracer_in[group * held : (group + 1) * held]
        blocks_out[group, held:] = metric_in[...]
        for side in range(2):
            halos_out[side, group] = halo_tile(group, side)

    peers = n * nlev - 1
    pl.semaphore_wait(
        barrier, peers + n * (has_low.astype(jnp.int32) + has_high.astype(jnp.int32))
    )

    mine = pl.ds(pl.multiple_of(px * nx, nx), nx)

    def block_copy(x):
        return pltpu.make_async_remote_copy(
            src_ref=blocks_out.at[x],
            dst_ref=blocks.at[:, mine, :],
            send_sem=block_send,
            recv_sem=block_recv,
            device_id=(x, py, lev),
            device_id_type=MESH,
        )

    def halo_copy(x, side):
        return pltpu.make_async_remote_copy(
            src_ref=halos_out.at[side, x],
            dst_ref=halos.at[side, mine, :],
            send_sem=halo_send.at[side],
            recv_sem=halo_recv.at[side],
            device_id=(x, py + (1 if side else -1), lev),
            device_id_type=MESH,
        )

    sides = ((0, has_low, has_high), (1, has_high, has_low))
    for x in others():
        block_copy(x).start()
    for side, sends, _ in sides:

        @pl.when(sends)
        def _(side=side):
            for x in everyone:
                halo_copy(x, side).start()

    blocks[:, mine, :] = blocks_out[px]
    for side, _, gets in sides:

        @pl.when(jnp.logical_not(gets))
        def _(side=side):
            halos[side] = jnp.zeros(halos.shape[1:], jnp.float32)

    def node_of(shape, axis):
        return lax.broadcasted_iota(jnp.int32, shape, axis)

    depth = ny + halos.shape[2]
    source = node_of((depth, 1), 0)
    slot = jnp.where(
        source < ny + width,
        reach + source // GLL_NODES,
        jnp.where(source < ny + 2 * width, (source - ny - width) // GLL_NODES, -SLOTS * GLL_NODES),
    )
    place = lax.rem(source, GLL_NODES) * SLOTS + slot
    column = node_of((1, spread.shape[1]), 1)
    spread[...] = jnp.where(place == column, 1.0, 0.0).astype(jnp.bfloat16)
    source = node_of((gather.shape[0], 1), 0)
    at = lax.rem(source, lanes)
    element = lax.rem(at, SLOTS) - reach
    kept = (element >= 0) & (element < elements_y) & (at // SLOTS < held)
    place = jnp.where(
        kept, at // SLOTS * ny + element * GLL_NODES + source // lanes, -1
    )
    gather[...] = jnp.where(place == node_of((1, gather.shape[1]), 1), 1.0, 0.0).astype(
        jnp.bfloat16
    )

    for side, _, gets in sides:

        @pl.when(gets)
        def _(side=side):
            took(halos.at[side], halo_recv.at[side])

    lane = lax.broadcasted_iota(jnp.int32, (elements_x, halos.shape[2]), 1)
    rows_of = [pl.ds(i, elements_x, stride=GLL_NODES) for i in range(GLL_NODES)]
    rims = []
    for rows in rows_of:
        high, low = halos[0, rows, :], halos[1, rows, :]
        rims.append(
            [
                jnp.where(
                    lane < width,
                    rolled(high, -width * k, 1),
                    jnp.where(lane < 2 * width, rolled(low, width - width * k, 1), 0.0),
                )
                for k in range(fields)
            ]
        )

    took(blocks.at[:, : (n - 1) * nx, :], block_recv)

    parts = [
        jnp.concatenate([blocks[k, rows_of[i], :], rims[i][k]], axis=1)
        for k in range(fields)
        for i in range(GLL_NODES)
    ]
    spread_out = moved_by_table(jnp.concatenate(parts, axis=0), spread[...])
    pair = 2 * SLOTS
    in_first = lax.broadcasted_iota(jnp.int32, (elements_x, pair), 1) < SLOTS

    def joined(first, second, i, j):
        first, second = (
            spread_out[
                (k * GLL_NODES + i) * elements_x : (k * GLL_NODES + i + 1) * elements_x,
                j // 2 * pair : (j // 2 + 1) * pair,
            ]
            for k in (first, second)
        )
        if j % 2:
            first = rolled(first, SLOTS, 1)
        else:
            second = rolled(second, SLOTS, 1)
        return jnp.where(in_first, first, second)

    def by_node(pairs):
        return [
            [
                jnp.concatenate([joined(first, second, i, j) for first, second in pairs], axis=1)
                for j in range(GLL_NODES)
            ]
            for i in range(GLL_NODES)
        ]

    tracer = by_node([(k, min(k + 1, held - 1)) for k in range(0, held, 2)])
    node_mass, wind_x, wind_y = (
        by_node([(held + k, held + k)] * (lanes // pair)) for k in range(3)
    )

    slot = lax.rem(lax.broadcasted_iota(jnp.int32, (elements_x, lanes), 1), SLOTS)
    element = py * elements_y + slot - reach
    inside = (slot < elements_y + 2 * reach) & (element >= 0) & (element < nz * elements_y)
    evolved = sections(tracer, node_mass, wind_x, wind_y, inside)

    evolved = moved_by_table(
        jnp.concatenate([jnp.concatenate(row, axis=1) for row in evolved], axis=0), gather[...]
    )
    for k in range(held):
        for i in range(GLL_NODES):
            results_out[k, pl.ds(i, elements_x, stride=GLL_NODES), :] = evolved[
                i * elements_x : (i + 1) * elements_x, k * ny : (k + 1) * ny
            ]

    holder = lax.rem(px, half)
    is_mine = target_lev == lev

    def result_copy(x):
        return pltpu.make_async_remote_copy(
            src_ref=results_out.at[:, pl.ds(pl.multiple_of(x * nx, nx), nx), :],
            dst_ref=results.at[lev, pl.ds(holder * held, held)],
            send_sem=result_send,
            recv_sem=result_recv,
            device_id=(x, py, target_lev),
            device_id_type=MESH,
        )

    for x in others():
        result_copy(x).start()

    @pl.when(jnp.logical_not(is_mine))
    def _():
        result_copy(px).start()
        took(results_out, result_recv)

    @pl.when(is_mine)
    def _():
        results[lev, pl.ds(holder * held, held)] = results_out[:, mine, :]
        took(results_out.at[:, : (n - 1) * nx, :], result_recv)

    remap_copy.wait()
    for a in range(nlev):
        total = remap[a, 0] * results[0]
        for b in range(1, nlev):
            total = total + remap[a, b] * results[b]
        out[a] = total

    took(blocks.at[:, : (n - 1) * nx, :], block_send)
    for side, sends, _ in sides:

        @pl.when(sends)
        def _(side=side):
            took(halos.at[side], halo_send.at[side])

    @pl.when(is_mine)
    def _():
        took(results_out.at[:, : (n - 1) * nx, :], result_send)

    @pl.when(jnp.logical_not(is_mine))
    def _():
        took(results_out, result_send)


def shards(n, nz, nlev, tracer, node_mass, wind_x, wind_y, remap):
    levels, tracers, nx, ny = tracer.shape
    held = tracers // n
    fields = held + 3
    reach = SECTION_REACH * len(section_weights)
    width = reach * GLL_NODES
    elements_y = ny // GLL_NODES
    if levels != 1 or tracers % n or n % nlev or nx % 8 or ny % 128:
        raise ValueError("unsupported split")
    if elements_y + 2 * reach > SLOTS or fields * width > 128 or width > ny:
        raise ValueError("unsupported block")
    lanes = -(-held * SLOTS // 128) * 128
    vmem, dma = pltpu.VMEM, pltpu.SemaphoreType.DMA
    f32 = jnp.float32
    anywhere = pl.BlockSpec(memory_space=pltpu.HBM)
    return pl.pallas_call(
        functools.partial(kernel, n, nz, nlev),
        out_shape=vmem((nlev, tracers // nlev, nx, ny), f32),
        in_specs=[anywhere] * 5,
        out_specs=pl.BlockSpec(memory_space=pltpu.VMEM),
        scratch_shapes=[
            vmem((tracers, nx, ny), f32),
            vmem((3, nx, ny), f32),
            pltpu.SMEM(remap.shape, f32),
            vmem((n, fields, nx, ny), f32),
            vmem((2, n, nx, 128), f32),
            vmem((fields, n * nx, ny), f32),
            vmem((2, n * nx, 128), f32),
            vmem((ny + 128, GLL_NODES * SLOTS), jnp.bfloat16),
            vmem((GLL_NODES * lanes, held * ny), jnp.bfloat16),
            vmem((held, n * nx, ny), f32),
            vmem((nlev, tracers // nlev, nx, ny), f32),
            dma((5,)),
            dma,
            dma,
            dma((2,)),
            dma((2,)),
            dma,
            dma,
        ],
        compiler_params=pltpu.CompilerParams(
            collective_id=0, has_side_effects=True, vmem_limit_bytes=32 * 1024 * 1024
        ),
        name="limited_step",
    )(
        *(
            pltpu.with_memory_space_constraint(operand, pltpu.HBM)
            for operand in (tracer, node_mass, wind_x, wind_y, remap)
        )
    )


def solution(mesh):
    sizes = [mesh.shape[axis] for axis in ("px", "py", "lev")]
    in_specs = (
        P("lev", None, "px", "py"),
        P("lev", "px", "py"),
        P("lev", "px", "py"),
        P("lev", "px", "py"),
        P(),
    )
    out_specs = P(None, "lev", "px", "py")
    return jax.shard_map(
        functools.partial(shards, *sizes),
        mesh=mesh,
        in_specs=in_specs,
        out_specs=out_specs,
        check_vma=False,
    )
```

```python
import functools

import jax
import jax.numpy as jnp
import numpy as np
from jax import lax
from jax.experimental import pallas as pl
from jax.experimental.pallas import tpu as pltpu
from jax.sharding import PartitionSpec as P

GLL_NODES = 4
SECTION_REACH = 2
SLOTS = 64

sentinel = 1e30
step_size = 0.1
section_weights = ((0.0, 1.0), (0.75, 0.25), (1.0 / 3.0, 2.0 / 3.0))
MESH = pl.DeviceIdType.MESH


def derivative_table():
    points = np.array([-1.0, -(5.0 ** (-0.5)), 5.0 ** (-0.5), 1.0])
    number = points.shape[0]
    barycentric = np.array(
        [
            1.0
            / np.prod([points[outer] - points[inner] for inner in range(number) if inner != outer])
            for outer in range(number)
        ]
    )
    table = np.zeros((number, number))
    for outer in range(number):
        for inner in range(number):
            if inner != outer:
                table[outer, inner] = (
                    barycentric[inner] / barycentric[outer] / (points[outer] - points[inner])
                )
    for outer in range(number):
        table[outer, outer] = -np.sum(table[outer])
    return table


def rolled(values, shift, axis):
    size = values.shape[axis]
    shift %= size
    return pltpu.roll(values, shift, axis) if shift else values


def moved_by_table(values, table):
    rows = values.shape[0]
    high = values.astype(jnp.bfloat16)
    low = (values - high.astype(jnp.float32)).astype(jnp.bfloat16)
    terms = jnp.dot(
        jnp.concatenate([high, low], axis=0), table, preferred_element_type=jnp.float32
    )
    return terms[:rows] + terms[rows:]


def sections(tracer, node_mass, wind_x, wind_y, inside):
    nodes = range(GLL_NODES)
    table = step_size * derivative_table()

    def node_sums(values):
        first = [values[0][j] + rolled(values[3][j], 1, 0) for j in nodes]
        last = [values[3][j] + rolled(values[0][j], -1, 0) for j in nodes]
        values = [first, values[1], values[2], last]
        return [
            [row[0] + rolled(row[3], 1, 1), row[1], row[2], row[3] + rolled(row[0], -1, 1)]
            for row in values
        ]

    def tree(combine, items):
        while len(items) > 1:
            items = [combine(*items[i : i + 2]) for i in range(0, len(items), 2)]
        return items[0]

    def around(combine, values):
        for axis in (0, 1):
            values = combine(
                combine(values, rolled(values, 1, axis)), rolled(values, -1, axis)
            )
        return values

    inverse = [
        [1.0 / jnp.where(inside, entry, 1.0) for entry in row] for row in node_sums(node_mass)
    ]
    field = tracer
    for share_start, share_new in section_weights:
        flat = [field[i][j] for i in nodes for j in nodes]
        lower = around(jnp.minimum, jnp.where(inside, tree(jnp.minimum, flat), sentinel))
        upper = around(jnp.maximum, jnp.where(inside, tree(jnp.maximum, flat), -sentinel))
        flux_x = [[wind_x[i][j] * field[i][j] for j in nodes] for i in nodes]
        flux_y = [[wind_y[i][j] * field[i][j] for j in nodes] for i in nodes]
        weighted = []
        for i in nodes:
            row = []
            for j in nodes:
                slope_x = tree(jnp.add, [float(table[i, k]) * flux_x[k][j] for k in nodes])
                slope_y = tree(jnp.add, [float(table[j, k]) * flux_y[i][k] for k in nodes])
                moved = field[i][j] - (slope_x + slope_y)
                limited = jnp.minimum(jnp.maximum(moved, lower), upper)
                row.append(node_mass[i][j] * limited)
            weighted.append(row)
        summed = node_sums(weighted)
        field = [
            [
                share_new * (summed[i][j] * inverse[i][j])
                + (share_start * tracer[i][j] if share_start else 0.0)
                for j in nodes
            ]
            for i in nodes
        ]
    return field


def kernel(
    n,
    nz,
    nlev,
    tracer_hbm,
    mass_hbm,
    wind_x_hbm,
    wind_y_hbm,
    remap_hbm,
    out,
    tracer_in,
    metric_in,
    remap,
    halos_out,
    blocks,
    halos,
    spread,
    gather,
    results_out,
    results,
    in_sem,
    block_send,
    block_recv,
    halo_send,
    halo_recv,
    result_send,
    result_recv,
):
    tracers, nx, ny = tracer_in.shape
    held = tracers // n
    fields = held + 3
    half = n // nlev
    reach = SECTION_REACH * len(section_weights)
    width = reach * GLL_NODES
    elements_y = ny // GLL_NODES
    elements_x = n * nx // GLL_NODES
    lanes = gather.shape[0] // GLL_NODES
    px, py, lev = lax.axis_index("px"), lax.axis_index("py"), lax.axis_index("lev")
    has_low, has_high = py > 0, py < nz - 1
    target_lev = px // half

    def others():
        return [lax.rem(px + d, n) for d in sorted(range(1, n), key=lambda d: abs(2 * d - n))]

    everyone = others() + [px]

    def took(ref, sem):
        pltpu.make_async_copy(ref, ref, sem).wait()

    barrier = pltpu.get_barrier_semaphore()

    def greet(x, y, level):
        pl.semaphore_signal(barrier, inc=1, device_id=(x, y, level), device_id_type=MESH)

    for near, there in ((has_low, py - 1), (has_high, py + 1)):

        @pl.when(near)
        def _(there=there):
            for x in everyone:
                greet(x, there, lev)

    for x in others():
        greet(x, py, lev)
    for x in everyone:
        for step in range(1, nlev):
            greet(x, py, lax.rem(lev + step, nlev))

    copies = [pltpu.make_async_copy(tracer_hbm.at[0], tracer_in, in_sem.at[0])]
    for k, source in enumerate((mass_hbm, wind_x_hbm, wind_y_hbm)):
        copies.append(pltpu.make_async_copy(source.at[0], metric_in.at[k], in_sem.at[k + 1]))
    remap_copy = pltpu.make_async_copy(remap_hbm, remap, in_sem.at[4])
    remap_copy.start()
    for copy in copies:
        copy.start()
    for copy in copies:
        copy.wait()


    lane = lax.broadcasted_iota(jnp.int32, (nx, halos.shape[2]), 1)

    def halo_tile(group, side):
        tile = jnp.zeros(lane.shape, jnp.float32)
        for k in range(fields):
            piece = tracer_in[group * held + k] if k < held else metric_in[k - held]
            shift = width * k - (ny - width if side else 0)
            wanted = (lane >= width * k) & (lane < width * (k + 1))
            tile = jnp.where(wanted, rolled(piece, shift, 1), tile)
        return tile

    for group in range(n):
        for side in range(2):
            halos_out[side, group] = halo_tile(group, side)

    peers = n * nlev - 1
    pl.semaphore_wait(
        barrier, peers + n * (has_low.astype(jnp.int32) + has_high.astype(jnp.int32))
    )

    mine = pl.ds(pl.multiple_of(px * nx, nx), nx)

    def block_copies(x):
        pieces = (
            (tracer_in.at[pl.ds(x * held, held)], blocks.at[:held, mine, :]),
            (metric_in, blocks.at[held:, mine, :]),
        )
        return [
            pltpu.make_async_remote_copy(
                src_ref=source,
                dst_ref=target,
                send_sem=block_send,
                recv_sem=block_recv,
                device_id=(x, py, lev),
                device_id_type=MESH,
            )
            for source, target in pieces
        ]

    def halo_copy(x, side):
        return pltpu.make_async_remote_copy(
            src_ref=halos_out.at[side, x],
            dst_ref=halos.at[side, mine, :],
            send_sem=halo_send.at[side],
            recv_sem=halo_recv.at[side],
            device_id=(x, py + (1 if side else -1), lev),
            device_id_type=MESH,
        )

    sides = ((0, has_low, has_high), (1, has_high, has_low))
    for x in others():
        for copy in block_copies(x):
            copy.start()
    for side, sends, _ in sides:

        @pl.when(sends)
        def _(side=side):
            for x in everyone:
                halo_copy(x, side).start()

    blocks[:held, mine, :] = tracer_in[pl.ds(px * held, held)]
    blocks[held:, mine, :] = metric_in[...]
    for side, _, gets in sides:

        @pl.when(jnp.logical_not(gets))
        def _(side=side):
            halos[side] = jnp.zeros(halos.shape[1:], jnp.float32)

    def node_of(shape, axis):
        return lax.broadcasted_iota(jnp.int32, shape, axis)

    depth = ny + halos.shape[2]
    source = node_of((depth, 1), 0)
    slot = jnp.where(
        source < ny + width,
        reach + source // GLL_NODES,
        jnp.where(source < ny + 2 * width, (source - ny - width) // GLL_NODES, -SLOTS * GLL_NODES),
    )
    place = lax.rem(source, GLL_NODES) * SLOTS + slot
    column = node_of((1, spread.shape[1]), 1)
    spread[...] = jnp.where(place == column, 1.0, 0.0).astype(jnp.bfloat16)
    source = node_of((gather.shape[0], 1), 0)
    at = lax.rem(source, lanes)
    element = lax.rem(at, SLOTS) - reach
    kept = (element >= 0) & (element < elements_y) & (at // SLOTS < held)
    place = jnp.where(
        kept, at // SLOTS * ny + element * GLL_NODES + source // lanes, -1
    )
    gather[...] = jnp.where(place == node_of((1, gather.shape[1]), 1), 1.0, 0.0).astype(
        jnp.bfloat16
    )

    for side, _, gets in sides:

        @pl.when(gets)
        def _(side=side):
            took(halos.at[side], halo_recv.at[side])

    lane = lax.broadcasted_iota(jnp.int32, (elements_x, halos.shape[2]), 1)
    rows_of = [pl.ds(i, elements_x, stride=GLL_NODES) for i in range(GLL_NODES)]
    rims = []
    for rows in rows_of:
        high, low = halos[0, rows, :], halos[1, rows, :]
        rims.append(
            [
                jnp.where(
                    lane < width,
                    rolled(high, -width * k, 1),
                    jnp.where(lane < 2 * width, rolled(low, width - width * k, 1), 0.0),
                )
                for k in range(fields)
            ]
        )

    took(blocks.at[:, : (n - 1) * nx, :], block_recv)

    parts = [
        jnp.concatenate([blocks[k, rows_of[i], :], rims[i][k]], axis=1)
        for k in range(fields)
        for i in range(GLL_NODES)
    ]
    spread_out = moved_by_table(jnp.concatenate(parts, axis=0), spread[...])
    pair = 2 * SLOTS
    in_first = lax.broadcasted_iota(jnp.int32, (elements_x, pair), 1) < SLOTS

    def joined(first, second, i, j):
        first, second = (
            spread_out[
                (k * GLL_NODES + i) * elements_x : (k * GLL_NODES + i + 1) * elements_x,
                j // 2 * pair : (j // 2 + 1) * pair,
            ]
            for k in (first, second)
        )
        if j % 2:
            first = rolled(first, SLOTS, 1)
        else:
            second = rolled(second, SLOTS, 1)
        return jnp.where(in_first, first, second)

    def by_node(pairs):
        return [
            [
                jnp.concatenate([joined(first, second, i, j) for first, second in pairs], axis=1)
                for j in range(GLL_NODES)
            ]
            for i in range(GLL_NODES)
        ]

    tracer = by_node([(k, min(k + 1, held - 1)) for k in range(0, held, 2)])
    node_mass, wind_x, wind_y = (
        by_node([(held + k, held + k)] * (lanes // pair)) for k in range(3)
    )

    slot = lax.rem(lax.broadcasted_iota(jnp.int32, (elements_x, lanes), 1), SLOTS)
    element = py * elements_y + slot - reach
    inside = (slot < elements_y + 2 * reach) & (element >= 0) & (element < nz * elements_y)
    evolved = sections(tracer, node_mass, wind_x, wind_y, inside)

    evolved = moved_by_table(
        jnp.concatenate([jnp.concatenate(row, axis=1) for row in evolved], axis=0), gather[...]
    )
    for k in range(held):
        for i in range(GLL_NODES):
            results_out[k, pl.ds(i, elements_x, stride=GLL_NODES), :] = evolved[
                i * elements_x : (i + 1) * elements_x, k * ny : (k + 1) * ny
            ]

    holder = lax.rem(px, half)
    is_mine = target_lev == lev

    def result_copy(x):
        return pltpu.make_async_remote_copy(
            src_ref=results_out.at[:, pl.ds(pl.multiple_of(x * nx, nx), nx), :],
            dst_ref=results.at[lev, pl.ds(holder * held, held)],
            send_sem=result_send,
            recv_sem=result_recv,
            device_id=(x, py, target_lev),
            device_id_type=MESH,
        )

    for x in others():
        result_copy(x).start()

    @pl.when(jnp.logical_not(is_mine))
    def _():
        result_copy(px).start()
        took(results_out, result_recv)

    @pl.when(is_mine)
    def _():
        results[lev, pl.ds(holder * held, held)] = results_out[:, mine, :]
        took(results_out.at[:, : (n - 1) * nx, :], result_recv)

    remap_copy.wait()
    for a in range(nlev):
        total = remap[a, 0] * results[0]
        for b in range(1, nlev):
            total = total + remap[a, b] * results[b]
        out[a] = total

    took(blocks.at[:, : (n - 1) * nx, :], block_send)
    for side, sends, _ in sides:

        @pl.when(sends)
        def _(side=side):
            took(halos.at[side], halo_send.at[side])

    @pl.when(is_mine)
    def _():
        took(results_out.at[:, : (n - 1) * nx, :], result_send)

    @pl.when(jnp.logical_not(is_mine))
    def _():
        took(results_out, result_send)


def shards(n, nz, nlev, tracer, node_mass, wind_x, wind_y, remap):
    levels, tracers, nx, ny = tracer.shape
    held = tracers // n
    fields = held + 3
    reach = SECTION_REACH * len(section_weights)
    width = reach * GLL_NODES
    elements_y = ny // GLL_NODES
    if levels != 1 or tracers % n or n % nlev or nx % 8 or ny % 128:
        raise ValueError("unsupported split")
    if elements_y + 2 * reach > SLOTS or fields * width > 128 or width > ny:
        raise ValueError("unsupported block")
    lanes = -(-held * SLOTS // 128) * 128
    vmem, dma = pltpu.VMEM, pltpu.SemaphoreType.DMA
    f32 = jnp.float32
    anywhere = pl.BlockSpec(memory_space=pltpu.HBM)
    return pl.pallas_call(
        functools.partial(kernel, n, nz, nlev),
        out_shape=vmem((nlev, tracers // nlev, nx, ny), f32),
        in_specs=[anywhere] * 5,
        out_specs=pl.BlockSpec(memory_space=pltpu.VMEM),
        scratch_shapes=[
            vmem((tracers, nx, ny), f32),
            vmem((3, nx, ny), f32),
            pltpu.SMEM(remap.shape, f32),
            vmem((2, n, nx, 128), f32),
            vmem((fields, n * nx, ny), f32),
            vmem((2, n * nx, 128), f32),
            vmem((ny + 128, GLL_NODES * SLOTS), jnp.bfloat16),
            vmem((GLL_NODES * lanes, held * ny), jnp.bfloat16),
            vmem((held, n * nx, ny), f32),
            vmem((nlev, tracers // nlev, nx, ny), f32),
            dma((5,)),
            dma,
            dma,
            dma((2,)),
            dma((2,)),
            dma,
            dma,
        ],
        compiler_params=pltpu.CompilerParams(
            collective_id=0, has_side_effects=True, vmem_limit_bytes=32 * 1024 * 1024
        ),
        name="limited_step",
    )(
        *(
            pltpu.with_memory_space_constraint(operand, pltpu.HBM)
            for operand in (tracer, node_mass, wind_x, wind_y, remap)
        )
    )


def solution(mesh):
    sizes = [mesh.shape[axis] for axis in ("px", "py", "lev")]
    in_specs = (
        P("lev", None, "px", "py"),
        P("lev", "px", "py"),
        P("lev", "px", "py"),
        P("lev", "px", "py"),
        P(),
    )
    out_specs = P(None, "lev", "px", "py")
    return jax.shard_map(
        functools.partial(shards, *sizes),
        mesh=mesh,
        in_specs=in_specs,
        out_specs=out_specs,
        check_vma=False,
    )
```

```python
import functools

import jax
import jax.numpy as jnp
import numpy as np
from jax import lax
from jax.experimental import pallas as pl
from jax.experimental.pallas import tpu as pltpu
from jax.sharding import PartitionSpec as P

GLL_NODES = 4
SECTION_REACH = 2
SLOTS = 64

sentinel = 1e30
step_size = 0.1
section_weights = ((0.0, 1.0), (0.75, 0.25), (1.0 / 3.0, 2.0 / 3.0))
MESH = pl.DeviceIdType.MESH


def derivative_table():
    points = np.array([-1.0, -(5.0 ** (-0.5)), 5.0 ** (-0.5), 1.0])
    number = points.shape[0]
    barycentric = np.array(
        [
            1.0
            / np.prod([points[outer] - points[inner] for inner in range(number) if inner != outer])
            for outer in range(number)
        ]
    )
    table = np.zeros((number, number))
    for outer in range(number):
        for inner in range(number):
            if inner != outer:
                table[outer, inner] = (
                    barycentric[inner] / barycentric[outer] / (points[outer] - points[inner])
                )
    for outer in range(number):
        table[outer, outer] = -np.sum(table[outer])
    return table


def rolled(values, shift, axis):
    size = values.shape[axis]
    shift %= size
    return pltpu.roll(values, shift, axis) if shift else values


def moved_by_table(values, table):
    rows = values.shape[0]
    high = values.astype(jnp.bfloat16)
    low = (values - high.astype(jnp.float32)).astype(jnp.bfloat16)
    terms = jnp.dot(
        jnp.concatenate([high, low], axis=0), table, preferred_element_type=jnp.float32
    )
    return terms[:rows] + terms[rows:]


def sections(tracer, node_mass, wind_x, wind_y, inside):
    nodes = range(GLL_NODES)
    table = step_size * derivative_table()

    def node_sums(values):
        first = [values[0][j] + rolled(values[3][j], 1, 0) for j in nodes]
        last = [values[3][j] + rolled(values[0][j], -1, 0) for j in nodes]
        values = [first, values[1], values[2], last]
        return [
            [row[0] + rolled(row[3], 1, 1), row[1], row[2], row[3] + rolled(row[0], -1, 1)]
            for row in values
        ]

    def tree(combine, items):
        while len(items) > 1:
            items = [combine(*items[i : i + 2]) for i in range(0, len(items), 2)]
        return items[0]

    def around(combine, values):
        for axis in (0, 1):
            values = combine(
                combine(values, rolled(values, 1, axis)), rolled(values, -1, axis)
            )
        return values

    inverse = [
        [1.0 / jnp.where(inside, entry, 1.0) for entry in row] for row in node_sums(node_mass)
    ]
    field = tracer
    for share_start, share_new in section_weights:
        flat = [field[i][j] for i in nodes for j in nodes]
        lower = around(jnp.minimum, jnp.where(inside, tree(jnp.minimum, flat), sentinel))
        upper = around(jnp.maximum, jnp.where(inside, tree(jnp.maximum, flat), -sentinel))
        flux_x = [[wind_x[i][j] * field[i][j] for j in nodes] for i in nodes]
        flux_y = [[wind_y[i][j] * field[i][j] for j in nodes] for i in nodes]
        weighted = []
        for i in nodes:
            row = []
            for j in nodes:
                slope_x = tree(jnp.add, [float(table[i, k]) * flux_x[k][j] for k in nodes])
                slope_y = tree(jnp.add, [float(table[j, k]) * flux_y[i][k] for k in nodes])
                moved = field[i][j] - (slope_x + slope_y)
                limited = jnp.minimum(jnp.maximum(moved, lower), upper)
                row.append(node_mass[i][j] * limited)
            weighted.append(row)
        summed = node_sums(weighted)
        field = [
            [
                share_new * (summed[i][j] * inverse[i][j])
                + (share_start * tracer[i][j] if share_start else 0.0)
                for j in nodes
            ]
            for i in nodes
        ]
    return field


def kernel(
    n,
    nz,
    nlev,
    tracer_hbm,
    mass_hbm,
    wind_x_hbm,
    wind_y_hbm,
    remap_hbm,
    out,
    tracer_in,
    metric_in,
    remap,
    halos_out,
    blocks,
    halos,
    spread,
    gather,
    results_out,
    results,
    in_sem,
    block_send,
    block_recv,
    halo_send,
    halo_recv,
    result_send,
    result_recv,
    ready,
):
    tracers, nx, ny = tracer_in.shape
    held = tracers // n
    fields = held + 3
    half = n // nlev
    reach = SECTION_REACH * len(section_weights)
    width = reach * GLL_NODES
    elements_y = ny // GLL_NODES
    elements_x = n * nx // GLL_NODES
    lanes = gather.shape[0] // GLL_NODES
    px, py, lev = lax.axis_index("px"), lax.axis_index("py"), lax.axis_index("lev")
    has_low, has_high = py > 0, py < nz - 1
    target_lev = px // half

    def others():
        return [d + (d >= px).astype(jnp.int32) for d in range(n - 1)]

    everyone = list(range(n))

    def took(ref, sem):
        pltpu.make_async_copy(ref, ref, sem).wait()

    barrier = pltpu.get_barrier_semaphore()

    def greet(x, y, level):
        pl.semaphore_signal(barrier, inc=1, device_id=(x, y, level), device_id_type=MESH)

    @pl.when(has_high)
    def _():
        for x in everyone:
            greet(x, py + 1, lev)

    for x in others():
        greet(x, py, lev)
    for x in everyone:
        for step in range(1, nlev):
            greet(x, py, lax.rem(lev + step, nlev))

    copies = [pltpu.make_async_copy(tracer_hbm.at[0], tracer_in, in_sem.at[0])]
    for k, source in enumerate((mass_hbm, wind_x_hbm, wind_y_hbm)):
        copies.append(pltpu.make_async_copy(source.at[0], metric_in.at[k], in_sem.at[k + 1]))
    remap_copy = pltpu.make_async_copy(remap_hbm, remap, in_sem.at[4])
    remap_copy.start()
    for copy in copies:
        copy.start()
    for copy in copies:
        copy.wait()


    lane = lax.broadcasted_iota(jnp.int32, (nx, halos.shape[2]), 1)

    def halo_tile(group, side):
        tile = jnp.zeros(lane.shape, jnp.float32)
        for k in range(fields):
            piece = tracer_in[group * held + k] if k < held else metric_in[k - held]
            shift = width * k - (ny - width if side else 0)
            wanted = (lane >= width * k) & (lane < width * (k + 1))
            tile = jnp.where(wanted, rolled(piece, shift, 1), tile)
        return tile

    for group in range(n):
        for side in range(2):
            halos_out[side, group] = halo_tile(group, side)

    peers = n * nlev - 1
    pl.semaphore_wait(barrier, peers + n * has_low.astype(jnp.int32))

    mine = pl.ds(pl.multiple_of(px * nx, nx), nx)

    def block_copies(x):
        pieces = (
            (tracer_in.at[pl.ds(x * held, held)], blocks.at[:held, mine, :]),
            (metric_in, blocks.at[held:, mine, :]),
        )
        return [
            pltpu.make_async_remote_copy(
                src_ref=source,
                dst_ref=target,
                send_sem=block_send,
                recv_sem=block_recv,
                device_id=(x, py, lev),
                device_id_type=MESH,
            )
            for source, target in pieces
        ]

    def halo_copy(x, side):
        return pltpu.make_async_remote_copy(
            src_ref=halos_out.at[side, x],
            dst_ref=halos.at[side, mine, :],
            send_sem=halo_send.at[side],
            recv_sem=halo_recv.at[side],
            device_id=(x, py + (1 if side else -1), lev),
            device_id_type=MESH,
        )

    sides = ((0, has_low, has_high), (1, has_high, has_low))
    @pl.when(has_low)
    def _():
        for x in everyone:
            halo_copy(x, 0).start()

    for x in others():
        for copy in block_copies(x):
            copy.start()

    @pl.when(has_low)
    def _():
        for x in everyone:
            pl.semaphore_signal(
                ready, inc=1, device_id=(x, py - 1, lev), device_id_type=MESH
            )

    blocks[:held, mine, :] = tracer_in[pl.ds(px * held, held)]
    blocks[held:, mine, :] = metric_in[...]
    for side, _, gets in sides:

        @pl.when(jnp.logical_not(gets))
        def _(side=side):
            halos[side] = jnp.zeros(halos.shape[1:], jnp.float32)

    def node_of(shape, axis):
        return lax.broadcasted_iota(jnp.int32, shape, axis)

    depth = ny + halos.shape[2]
    source = node_of((depth, 1), 0)
    slot = jnp.where(
        source < ny + width,
        reach + source // GLL_NODES,
        jnp.where(source < ny + 2 * width, (source - ny - width) // GLL_NODES, -SLOTS * GLL_NODES),
    )
    place = lax.rem(source, GLL_NODES) * SLOTS + slot
    column = node_of((1, spread.shape[1]), 1)
    spread[...] = jnp.where(place == column, 1.0, 0.0).astype(jnp.bfloat16)
    source = node_of((gather.shape[0], 1), 0)
    at = lax.rem(source, lanes)
    element = lax.rem(at, SLOTS) - reach
    kept = (element >= 0) & (element < elements_y) & (at // SLOTS < held)
    place = jnp.where(
        kept, at // SLOTS * ny + element * GLL_NODES + source // lanes, -1
    )
    gather[...] = jnp.where(place == node_of((1, gather.shape[1]), 1), 1.0, 0.0).astype(
        jnp.bfloat16
    )

    @pl.when(has_high)
    def _():
        pl.semaphore_wait(ready, n)
        for x in everyone:
            halo_copy(x, 1).start()

    for side, _, gets in sides:

        @pl.when(gets)
        def _(side=side):
            took(halos.at[side], halo_recv.at[side])

    lane = lax.broadcasted_iota(jnp.int32, (elements_x, halos.shape[2]), 1)
    rows_of = [pl.ds(i, elements_x, stride=GLL_NODES) for i in range(GLL_NODES)]
    rims = []
    for rows in rows_of:
        high, low = halos[0, rows, :], halos[1, rows, :]
        rims.append(
            [
                jnp.where(
                    lane < width,
                    rolled(high, -width * k, 1),
                    jnp.where(lane < 2 * width, rolled(low, width - width * k, 1), 0.0),
                )
                for k in range(fields)
            ]
        )

    took(blocks.at[:, : (n - 1) * nx, :], block_recv)

    parts = [
        jnp.concatenate([blocks[k, rows_of[i], :], rims[i][k]], axis=1)
        for k in range(fields)
        for i in range(GLL_NODES)
    ]
    spread_out = moved_by_table(jnp.concatenate(parts, axis=0), spread[...])
    pair = 2 * SLOTS
    in_first = lax.broadcasted_iota(jnp.int32, (elements_x, pair), 1) < SLOTS

    def joined(first, second, i, j):
        first, second = (
            spread_out[
                (k * GLL_NODES + i) * elements_x : (k * GLL_NODES + i + 1) * elements_x,
                j // 2 * pair : (j // 2 + 1) * pair,
            ]
            for k in (first, second)
        )
        if j % 2:
            first = rolled(first, SLOTS, 1)
        else:
            second = rolled(second, SLOTS, 1)
        return jnp.where(in_first, first, second)

    def by_node(pairs):
        return [
            [
                jnp.concatenate([joined(first, second, i, j) for first, second in pairs], axis=1)
                for j in range(GLL_NODES)
            ]
            for i in range(GLL_NODES)
        ]

    tracer = by_node([(k, min(k + 1, held - 1)) for k in range(0, held, 2)])
    node_mass, wind_x, wind_y = (
        by_node([(held + k, held + k)] * (lanes // pair)) for k in range(3)
    )

    slot = lax.rem(lax.broadcasted_iota(jnp.int32, (elements_x, lanes), 1), SLOTS)
    element = py * elements_y + slot - reach
    inside = (slot < elements_y + 2 * reach) & (element >= 0) & (element < nz * elements_y)
    evolved = sections(tracer, node_mass, wind_x, wind_y, inside)

    evolved = moved_by_table(
        jnp.concatenate([jnp.concatenate(row, axis=1) for row in evolved], axis=0), gather[...]
    )
    for k in range(held):
        for i in range(GLL_NODES):
            results_out[k, pl.ds(i, elements_x, stride=GLL_NODES), :] = evolved[
                i * elements_x : (i + 1) * elements_x, k * ny : (k + 1) * ny
            ]

    holder = lax.rem(px, half)
    is_mine = target_lev == lev

    def result_copy(x):
        return pltpu.make_async_remote_copy(
            src_ref=results_out.at[:, pl.ds(pl.multiple_of(x * nx, nx), nx), :],
            dst_ref=results.at[lev, pl.ds(holder * held, held)],
            send_sem=result_send,
            recv_sem=result_recv,
            device_id=(x, py, target_lev),
            device_id_type=MESH,
        )

    @pl.when(jnp.logical_not(is_mine))
    def _():
        for x in everyone:
            result_copy(x).start()
        took(results_out, result_recv)

    @pl.when(is_mine)
    def _():
        for x in others():
            result_copy(x).start()
        results[lev, pl.ds(holder * held, held)] = results_out[:, mine, :]
        took(results_out.at[:, : (n - 1) * nx, :], result_recv)

    remap_copy.wait()
    for a in range(nlev):
        total = remap[a, 0] * results[0]
        for b in range(1, nlev):
            total = total + remap[a, b] * results[b]
        out[a] = total

    took(blocks.at[:, : (n - 1) * nx, :], block_send)
    for side, sends, _ in sides:

        @pl.when(sends)
        def _(side=side):
            took(halos.at[side], halo_send.at[side])

    @pl.when(is_mine)
    def _():
        took(results_out.at[:, : (n - 1) * nx, :], result_send)

    @pl.when(jnp.logical_not(is_mine))
    def _():
        took(results_out, result_send)


def shards(n, nz, nlev, tracer, node_mass, wind_x, wind_y, remap):
    levels, tracers, nx, ny = tracer.shape
    held = tracers // n
    fields = held + 3
    reach = SECTION_REACH * len(section_weights)
    width = reach * GLL_NODES
    elements_y = ny // GLL_NODES
    if levels != 1 or tracers % n or n % nlev or nx % 8 or ny % 128:
        raise ValueError("unsupported split")
    if elements_y + 2 * reach > SLOTS or fields * width > 128 or width > ny:
        raise ValueError("unsupported block")
    lanes = -(-held * SLOTS // 128) * 128
    vmem, dma = pltpu.VMEM, pltpu.SemaphoreType.DMA
    f32 = jnp.float32
    anywhere = pl.BlockSpec(memory_space=pltpu.HBM)
    return pl.pallas_call(
        functools.partial(kernel, n, nz, nlev),
        out_shape=vmem((nlev, tracers // nlev, nx, ny), f32),
        in_specs=[anywhere] * 5,
        out_specs=pl.BlockSpec(memory_space=pltpu.VMEM),
        scratch_shapes=[
            vmem((tracers, nx, ny), f32),
            vmem((3, nx, ny), f32),
            pltpu.SMEM(remap.shape, f32),
            vmem((2, n, nx, 128), f32),
            vmem((fields, n * nx, ny), f32),
            vmem((2, n * nx, 128), f32),
            vmem((ny + 128, GLL_NODES * SLOTS), jnp.bfloat16),
            vmem((GLL_NODES * lanes, held * ny), jnp.bfloat16),
            vmem((held, n * nx, ny), f32),
            vmem((nlev, tracers // nlev, nx, ny), f32),
            dma((5,)),
            dma,
            dma,
            dma((2,)),
            dma((2,)),
            dma,
            dma,
            pltpu.SemaphoreType.REGULAR,
        ],
        compiler_params=pltpu.CompilerParams(
            collective_id=0, has_side_effects=True, vmem_limit_bytes=32 * 1024 * 1024
        ),
        name="limited_step",
    )(
        *(
            pltpu.with_memory_space_constraint(operand, pltpu.HBM)
            for operand in (tracer, node_mass, wind_x, wind_y, remap)
        )
    )


def solution(mesh):
    sizes = [mesh.shape[axis] for axis in ("px", "py", "lev")]
    in_specs = (
        P("lev", None, "px", "py"),
        P("lev", "px", "py"),
        P("lev", "px", "py"),
        P("lev", "px", "py"),
        P(),
    )
    out_specs = P(None, "lev", "px", "py")
    return jax.shard_map(
        functools.partial(shards, *sizes),
        mesh=mesh,
        in_specs=in_specs,
        out_specs=out_specs,
        check_vma=False,
    )
```

```python
import functools

import jax
import jax.numpy as jnp
import numpy as np
from jax import lax
from jax.experimental import pallas as pl
from jax.experimental.pallas import tpu as pltpu
from jax.sharding import PartitionSpec as P

GLL_NODES = 4
SECTION_REACH = 2
SLOTS = 64

sentinel = 1e30
step_size = 0.1
section_weights = ((0.0, 1.0), (0.75, 0.25), (1.0 / 3.0, 2.0 / 3.0))
MESH = pl.DeviceIdType.MESH


def derivative_table():
    points = np.array([-1.0, -(5.0 ** (-0.5)), 5.0 ** (-0.5), 1.0])
    number = points.shape[0]
    barycentric = np.array(
        [
            1.0
            / np.prod([points[outer] - points[inner] for inner in range(number) if inner != outer])
            for outer in range(number)
        ]
    )
    table = np.zeros((number, number))
    for outer in range(number):
        for inner in range(number):
            if inner != outer:
                table[outer, inner] = (
                    barycentric[inner] / barycentric[outer] / (points[outer] - points[inner])
                )
    for outer in range(number):
        table[outer, outer] = -np.sum(table[outer])
    return table


def rolled(values, shift, axis):
    size = values.shape[axis]
    shift %= size
    return pltpu.roll(values, shift, axis) if shift else values


def moved_by_table(values, table):
    rows = values.shape[0]
    high = values.astype(jnp.bfloat16)
    low = (values - high.astype(jnp.float32)).astype(jnp.bfloat16)
    terms = jnp.dot(
        jnp.concatenate([high, low], axis=0), table, preferred_element_type=jnp.float32
    )
    return terms[:rows] + terms[rows:]


def sections(tracer, node_mass, wind_x, wind_y, inside):
    nodes = range(GLL_NODES)
    table = step_size * derivative_table()

    def node_sums(values):
        first = [values[0][j] + rolled(values[3][j], 1, 0) for j in nodes]
        last = [values[3][j] + rolled(values[0][j], -1, 0) for j in nodes]
        values = [first, values[1], values[2], last]
        return [
            [row[0] + rolled(row[3], 1, 1), row[1], row[2], row[3] + rolled(row[0], -1, 1)]
            for row in values
        ]

    def tree(combine, items):
        while len(items) > 1:
            items = [combine(*items[i : i + 2]) for i in range(0, len(items), 2)]
        return items[0]

    def around(combine, values):
        for axis in (0, 1):
            values = combine(
                combine(values, rolled(values, 1, axis)), rolled(values, -1, axis)
            )
        return values

    inverse = [
        [1.0 / jnp.where(inside, entry, 1.0) for entry in row] for row in node_sums(node_mass)
    ]
    field = tracer
    for share_start, share_new in section_weights:
        flat = [field[i][j] for i in nodes for j in nodes]
        lower = around(jnp.minimum, jnp.where(inside, tree(jnp.minimum, flat), sentinel))
        upper = around(jnp.maximum, jnp.where(inside, tree(jnp.maximum, flat), -sentinel))
        flux_x = [[wind_x[i][j] * field[i][j] for j in nodes] for i in nodes]
        flux_y = [[wind_y[i][j] * field[i][j] for j in nodes] for i in nodes]
        weighted = []
        for i in nodes:
            row = []
            for j in nodes:
                slope_x = tree(jnp.add, [float(table[i, k]) * flux_x[k][j] for k in nodes])
                slope_y = tree(jnp.add, [float(table[j, k]) * flux_y[i][k] for k in nodes])
                moved = field[i][j] - (slope_x + slope_y)
                limited = jnp.minimum(jnp.maximum(moved, lower), upper)
                row.append(node_mass[i][j] * limited)
            weighted.append(row)
        summed = node_sums(weighted)
        field = [
            [
                share_new * (summed[i][j] * inverse[i][j])
                + (share_start * tracer[i][j] if share_start else 0.0)
                for j in nodes
            ]
            for i in nodes
        ]
    return field


def kernel(
    n,
    nz,
    nlev,
    tracer_hbm,
    mass_hbm,
    wind_x_hbm,
    wind_y_hbm,
    remap_hbm,
    out,
    tracer_in,
    metric_in,
    remap,
    halos_out,
    blocks,
    halos,
    spread,
    gather,
    results_out,
    results,
    in_sem,
    block_send,
    block_recv,
    halo_send,
    halo_recv,
    result_send,
    result_recv,
    ready,
):
    tracers, nx, ny = tracer_in.shape
    held = tracers // n
    fields = held + 3
    half = n // nlev
    reach = SECTION_REACH * len(section_weights)
    width = reach * GLL_NODES
    elements_y = ny // GLL_NODES
    elements_x = n * nx // GLL_NODES
    lanes = gather.shape[0] // GLL_NODES
    px, py, lev = lax.axis_index("px"), lax.axis_index("py"), lax.axis_index("lev")
    has_low, has_high = py > 0, py < nz - 1
    target_lev = px // half

    def others():
        return [d + (d >= px).astype(jnp.int32) for d in range(n - 1)]

    everyone = list(range(n))

    def took(ref, sem):
        pltpu.make_async_copy(ref, ref, sem).wait()

    barrier = pltpu.get_barrier_semaphore()

    def greet(x, y, level):
        pl.semaphore_signal(barrier, inc=1, device_id=(x, y, level), device_id_type=MESH)

    @pl.when(has_high)
    def _():
        for x in everyone:
            greet(x, py + 1, lev)

    for x in others():
        greet(x, py, lev)
    for x in everyone:
        for step in range(1, nlev):
            greet(x, py, lax.rem(lev + step, nlev))

    copies = [pltpu.make_async_copy(tracer_hbm.at[0], tracer_in, in_sem.at[0])]
    for k, source in enumerate((mass_hbm, wind_x_hbm, wind_y_hbm)):
        copies.append(pltpu.make_async_copy(source.at[0], metric_in.at[k], in_sem.at[k + 1]))
    remap_copy = pltpu.make_async_copy(remap_hbm, remap, in_sem.at[4])
    remap_copy.start()
    for copy in copies:
        copy.start()

    peers = n * nlev - 1
    pl.semaphore_wait(barrier, peers + n * has_low.astype(jnp.int32))

    @pl.when(has_low)
    def _():
        for x in everyone:
            pl.semaphore_signal(
                ready, inc=1, device_id=(x, py - 1, lev), device_id_type=MESH
            )

    for copy in copies:
        copy.wait()

    lane = lax.broadcasted_iota(jnp.int32, (nx, halos.shape[2]), 1)

    def halo_tile(group, side):
        tile = jnp.zeros(lane.shape, jnp.float32)
        for k in range(fields):
            piece = tracer_in[group * held + k] if k < held else metric_in[k - held]
            shift = width * k - (ny - width if side else 0)
            wanted = (lane >= width * k) & (lane < width * (k + 1))
            tile = jnp.where(wanted, rolled(piece, shift, 1), tile)
        return tile

    for group in range(n):
        halos_out[0, group] = halo_tile(group, 0)

    mine = pl.ds(pl.multiple_of(px * nx, nx), nx)

    def block_copies(x):
        pieces = (
            (tracer_in.at[pl.ds(x * held, held)], blocks.at[:held, mine, :]),
            (metric_in, blocks.at[held:, mine, :]),
        )
        return [
            pltpu.make_async_remote_copy(
                src_ref=source,
                dst_ref=target,
                send_sem=block_send,
                recv_sem=block_recv,
                device_id=(x, py, lev),
                device_id_type=MESH,
            )
            for source, target in pieces
        ]

    def halo_copy(x, side):
        return pltpu.make_async_remote_copy(
            src_ref=halos_out.at[side, x],
            dst_ref=halos.at[side, mine, :],
            send_sem=halo_send.at[side],
            recv_sem=halo_recv.at[side],
            device_id=(x, py + (1 if side else -1), lev),
            device_id_type=MESH,
        )

    sides = ((0, has_low, has_high), (1, has_high, has_low))

    @pl.when(has_low)
    def _():
        for x in everyone:
            halo_copy(x, 0).start()

    for x in others():
        for copy in block_copies(x):
            copy.start()

    for group in range(n):
        halos_out[1, group] = halo_tile(group, 1)

    @pl.when(has_high)
    def _():
        pl.semaphore_wait(ready, n)
        for x in everyone:
            halo_copy(x, 1).start()

    blocks[:held, mine, :] = tracer_in[pl.ds(px * held, held)]
    blocks[held:, mine, :] = metric_in[...]
    for side, _, gets in sides:

        @pl.when(jnp.logical_not(gets))
        def _(side=side):
            halos[side] = jnp.zeros(halos.shape[1:], jnp.float32)

    def node_of(shape, axis):
        return lax.broadcasted_iota(jnp.int32, shape, axis)

    depth = ny + halos.shape[2]
    source = node_of((depth, 1), 0)
    slot = jnp.where(
        source < ny + width,
        reach + source // GLL_NODES,
        jnp.where(source < ny + 2 * width, (source - ny - width) // GLL_NODES, -SLOTS * GLL_NODES),
    )
    place = lax.rem(source, GLL_NODES) * SLOTS + slot
    column = node_of((1, spread.shape[1]), 1)
    spread[...] = jnp.where(place == column, 1.0, 0.0).astype(jnp.bfloat16)
    source = node_of((gather.shape[0], 1), 0)
    at = lax.rem(source, lanes)
    element = lax.rem(at, SLOTS) - reach
    kept = (element >= 0) & (element < elements_y) & (at // SLOTS < held)
    place = jnp.where(
        kept, at // SLOTS * ny + element * GLL_NODES + source // lanes, -1
    )
    gather[...] = jnp.where(place == node_of((1, gather.shape[1]), 1), 1.0, 0.0).astype(
        jnp.bfloat16
    )

    for side, _, gets in sides:

        @pl.when(gets)
        def _(side=side):
            took(halos.at[side], halo_recv.at[side])

    lane = lax.broadcasted_iota(jnp.int32, (elements_x, halos.shape[2]), 1)
    rows_of = [pl.ds(i, elements_x, stride=GLL_NODES) for i in range(GLL_NODES)]
    rims = []
    for rows in rows_of:
        high, low = halos[0, rows, :], halos[1, rows, :]
        rims.append(
            [
                jnp.where(
                    lane < width,
                    rolled(high, -width * k, 1),
                    jnp.where(lane < 2 * width, rolled(low, width - width * k, 1), 0.0),
                )
                for k in range(fields)
            ]
        )

    took(blocks.at[:, : (n - 1) * nx, :], block_recv)

    parts = [
        jnp.concatenate([blocks[k, rows_of[i], :], rims[i][k]], axis=1)
        for k in range(fields)
        for i in range(GLL_NODES)
    ]
    spread_out = moved_by_table(jnp.concatenate(parts, axis=0), spread[...])
    pair = 2 * SLOTS
    in_first = lax.broadcasted_iota(jnp.int32, (elements_x, pair), 1) < SLOTS

    def joined(first, second, i, j):
        first, second = (
            spread_out[
                (k * GLL_NODES + i) * elements_x : (k * GLL_NODES + i + 1) * elements_x,
                j // 2 * pair : (j // 2 + 1) * pair,
            ]
            for k in (first, second)
        )
        if j % 2:
            first = rolled(first, SLOTS, 1)
        else:
            second = rolled(second, SLOTS, 1)
        return jnp.where(in_first, first, second)

    def by_node(pairs):
        return [
            [
                jnp.concatenate([joined(first, second, i, j) for first, second in pairs], axis=1)
                for j in range(GLL_NODES)
            ]
            for i in range(GLL_NODES)
        ]

    tracer = by_node([(k, min(k + 1, held - 1)) for k in range(0, held, 2)])
    node_mass, wind_x, wind_y = (
        by_node([(held + k, held + k)] * (lanes // pair)) for k in range(3)
    )

    slot = lax.rem(lax.broadcasted_iota(jnp.int32, (elements_x, lanes), 1), SLOTS)
    element = py * elements_y + slot - reach
    inside = (slot < elements_y + 2 * reach) & (element >= 0) & (element < nz * elements_y)
    evolved = sections(tracer, node_mass, wind_x, wind_y, inside)

    evolved = moved_by_table(
        jnp.concatenate([jnp.concatenate(row, axis=1) for row in evolved], axis=0), gather[...]
    )
    for k in range(held):
        for i in range(GLL_NODES):
            results_out[k, pl.ds(i, elements_x, stride=GLL_NODES), :] = evolved[
                i * elements_x : (i + 1) * elements_x, k * ny : (k + 1) * ny
            ]

    holder = lax.rem(px, half)
    is_mine = target_lev == lev

    def result_copy(x):
        return pltpu.make_async_remote_copy(
            src_ref=results_out.at[:, pl.ds(pl.multiple_of(x * nx, nx), nx), :],
            dst_ref=results.at[lev, pl.ds(holder * held, held)],
            send_sem=result_send,
            recv_sem=result_recv,
            device_id=(x, py, target_lev),
            device_id_type=MESH,
        )

    @pl.when(jnp.logical_not(is_mine))
    def _():
        for x in everyone:
            result_copy(x).start()
        took(results_out, result_recv)

    @pl.when(is_mine)
    def _():
        for x in others():
            result_copy(x).start()
        results[lev, pl.ds(holder * held, held)] = results_out[:, mine, :]
        took(results_out.at[:, : (n - 1) * nx, :], result_recv)

    remap_copy.wait()
    for a in range(nlev):
        total = remap[a, 0] * results[0]
        for b in range(1, nlev):
            total = total + remap[a, b] * results[b]
        out[a] = total

    took(blocks.at[:, : (n - 1) * nx, :], block_send)
    for side, sends, _ in sides:

        @pl.when(sends)
        def _(side=side):
            took(halos.at[side], halo_send.at[side])

    @pl.when(is_mine)
    def _():
        took(results_out.at[:, : (n - 1) * nx, :], result_send)

    @pl.when(jnp.logical_not(is_mine))
    def _():
        took(results_out, result_send)


def shards(n, nz, nlev, tracer, node_mass, wind_x, wind_y, remap):
    levels, tracers, nx, ny = tracer.shape
    held = tracers // n
    fields = held + 3
    reach = SECTION_REACH * len(section_weights)
    width = reach * GLL_NODES
    elements_y = ny // GLL_NODES
    if levels != 1 or tracers % n or n % nlev or nx % 8 or ny % 128:
        raise ValueError("unsupported split")
    if elements_y + 2 * reach > SLOTS or fields * width > 128 or width > ny:
        raise ValueError("unsupported block")
    lanes = -(-held * SLOTS // 128) * 128
    vmem, dma = pltpu.VMEM, pltpu.SemaphoreType.DMA
    f32 = jnp.float32
    anywhere = pl.BlockSpec(memory_space=pltpu.HBM)
    return pl.pallas_call(
        functools.partial(kernel, n, nz, nlev),
        out_shape=vmem((nlev, tracers // nlev, nx, ny), f32),
        in_specs=[anywhere] * 5,
        out_specs=pl.BlockSpec(memory_space=pltpu.VMEM),
        scratch_shapes=[
            vmem((tracers, nx, ny), f32),
            vmem((3, nx, ny), f32),
            pltpu.SMEM(remap.shape, f32),
            vmem((2, n, nx, 128), f32),
            vmem((fields, n * nx, ny), f32),
            vmem((2, n * nx, 128), f32),
            vmem((ny + 128, GLL_NODES * SLOTS), jnp.bfloat16),
            vmem((GLL_NODES * lanes, held * ny), jnp.bfloat16),
            vmem((held, n * nx, ny), f32),
            vmem((nlev, tracers // nlev, nx, ny), f32),
            dma((5,)),
            dma,
            dma,
            dma((2,)),
            dma((2,)),
            dma,
            dma,
            pltpu.SemaphoreType.REGULAR,
        ],
        compiler_params=pltpu.CompilerParams(
            collective_id=0, has_side_effects=True, vmem_limit_bytes=32 * 1024 * 1024
        ),
        name="limited_step",
    )(
        *(
            pltpu.with_memory_space_constraint(operand, pltpu.HBM)
            for operand in (tracer, node_mass, wind_x, wind_y, remap)
        )
    )


def solution(mesh):
    sizes = [mesh.shape[axis] for axis in ("px", "py", "lev")]
    in_specs = (
        P("lev", None, "px", "py"),
        P("lev", "px", "py"),
        P("lev", "px", "py"),
        P("lev", "px", "py"),
        P(),
    )
    out_specs = P(None, "lev", "px", "py")
    return jax.shard_map(
        functools.partial(shards, *sizes),
        mesh=mesh,
        in_specs=in_specs,
        out_specs=out_specs,
        check_vma=False,
    )
```

```python
import functools

import jax
import jax.numpy as jnp
import numpy as np
from jax import lax
from jax.experimental import pallas as pl
from jax.experimental.pallas import tpu as pltpu
from jax.sharding import PartitionSpec as P

GLL_NODES = 4
SECTION_REACH = 2
SLOTS = 64

sentinel = 1e30
step_size = 0.1
section_weights = ((0.0, 1.0), (0.75, 0.25), (1.0 / 3.0, 2.0 / 3.0))
MESH = pl.DeviceIdType.MESH


def derivative_table():
    points = np.array([-1.0, -(5.0 ** (-0.5)), 5.0 ** (-0.5), 1.0])
    number = points.shape[0]
    barycentric = np.array(
        [
            1.0
            / np.prod([points[outer] - points[inner] for inner in range(number) if inner != outer])
            for outer in range(number)
        ]
    )
    table = np.zeros((number, number))
    for outer in range(number):
        for inner in range(number):
            if inner != outer:
                table[outer, inner] = (
                    barycentric[inner] / barycentric[outer] / (points[outer] - points[inner])
                )
    for outer in range(number):
        table[outer, outer] = -np.sum(table[outer])
    return table


def rolled(values, shift, axis):
    size = values.shape[axis]
    shift %= size
    return pltpu.roll(values, shift, axis) if shift else values


def moved_by_table(values, table):
    rows = values.shape[0]
    high = values.astype(jnp.bfloat16)
    low = (values - high.astype(jnp.float32)).astype(jnp.bfloat16)
    terms = jnp.dot(
        jnp.concatenate([high, low], axis=0), table, preferred_element_type=jnp.float32
    )
    return terms[:rows] + terms[rows:]


def sections(tracer, node_mass, wind_x, wind_y, inside):
    nodes = range(GLL_NODES)
    table = step_size * derivative_table()

    def node_sums(values):
        first = [values[0][j] + rolled(values[3][j], 1, 0) for j in nodes]
        last = [values[3][j] + rolled(values[0][j], -1, 0) for j in nodes]
        values = [first, values[1], values[2], last]
        return [
            [row[0] + rolled(row[3], 1, 1), row[1], row[2], row[3] + rolled(row[0], -1, 1)]
            for row in values
        ]

    def tree(combine, items):
        while len(items) > 1:
            items = [combine(*items[i : i + 2]) for i in range(0, len(items), 2)]
        return items[0]

    def around(combine, values):
        for axis in (0, 1):
            values = combine(
                combine(values, rolled(values, 1, axis)), rolled(values, -1, axis)
            )
        return values

    inverse = [
        [1.0 / jnp.where(inside, entry, 1.0) for entry in row] for row in node_sums(node_mass)
    ]
    field = tracer
    for share_start, share_new in section_weights:
        flat = [field[i][j] for i in nodes for j in nodes]
        lower = around(jnp.minimum, jnp.where(inside, tree(jnp.minimum, flat), sentinel))
        upper = around(jnp.maximum, jnp.where(inside, tree(jnp.maximum, flat), -sentinel))
        flux_x = [[wind_x[i][j] * field[i][j] for j in nodes] for i in nodes]
        flux_y = [[wind_y[i][j] * field[i][j] for j in nodes] for i in nodes]
        weighted = []
        for i in nodes:
            row = []
            for j in nodes:
                slope_x = tree(jnp.add, [float(table[i, k]) * flux_x[k][j] for k in nodes])
                slope_y = tree(jnp.add, [float(table[j, k]) * flux_y[i][k] for k in nodes])
                moved = field[i][j] - (slope_x + slope_y)
                limited = jnp.minimum(jnp.maximum(moved, lower), upper)
                row.append(node_mass[i][j] * limited)
            weighted.append(row)
        summed = node_sums(weighted)
        field = [
            [
                share_new * (summed[i][j] * inverse[i][j])
                + (share_start * tracer[i][j] if share_start else 0.0)
                for j in nodes
            ]
            for i in nodes
        ]
    return field


def kernel(
    n,
    nz,
    nlev,
    tracer_hbm,
    mass_hbm,
    wind_x_hbm,
    wind_y_hbm,
    remap_hbm,
    out,
    tracer_in,
    metric_in,
    remap,
    halos_out,
    blocks,
    halos,
    spread,
    gather,
    results_out,
    results,
    in_sem,
    block_send,
    block_recv,
    halo_send,
    halo_recv,
    result_send,
    result_recv,
    ready,
):
    tracers, nx, ny = tracer_in.shape
    held = tracers // n
    fields = held + 3
    half = n // nlev
    reach = SECTION_REACH * len(section_weights)
    width = reach * GLL_NODES
    elements_y = ny // GLL_NODES
    elements_x = n * nx // GLL_NODES
    lanes = gather.shape[0] // GLL_NODES
    px, py, lev = lax.axis_index("px"), lax.axis_index("py"), lax.axis_index("lev")
    has_low, has_high = py > 0, py < nz - 1
    target_lev = px // half

    def others():
        return [d + (d >= px).astype(jnp.int32) for d in range(n - 1)]

    everyone = list(range(n))

    def took(ref, sem):
        pltpu.make_async_copy(ref, ref, sem).wait()

    copies = [pltpu.make_async_copy(tracer_hbm.at[0], tracer_in, in_sem.at[0])]
    for k, source in enumerate((mass_hbm, wind_x_hbm, wind_y_hbm)):
        copies.append(pltpu.make_async_copy(source.at[0], metric_in.at[k], in_sem.at[k + 1]))
    remap_copy = pltpu.make_async_copy(remap_hbm, remap, in_sem.at[4])
    for copy in copies:
        copy.start()

    barrier = pltpu.get_barrier_semaphore()

    def greet(x, y, level):
        pl.semaphore_signal(barrier, inc=1, device_id=(x, y, level), device_id_type=MESH)

    for x in others():
        greet(x, py, lev)
    for x in everyone:
        for step in range(1, nlev):
            greet(x, py, lax.rem(lev + step, nlev))

    @pl.when(has_high)
    def _():
        for x in everyone:
            greet(x, py + 1, lev)

    peers = n * nlev - 1
    pl.semaphore_wait(barrier, peers + n * has_low.astype(jnp.int32))

    @pl.when(has_low)
    def _():
        for x in everyone:
            pl.semaphore_signal(
                ready, inc=1, device_id=(x, py - 1, lev), device_id_type=MESH
            )

    remap_copy.start()
    for copy in copies:
        copy.wait()

    lane = lax.broadcasted_iota(jnp.int32, (nx, halos.shape[2]), 1)

    def halo_tile(group, side):
        tile = jnp.zeros(lane.shape, jnp.float32)
        for k in range(fields):
            piece = tracer_in[group * held + k] if k < held else metric_in[k - held]
            shift = width * k - (ny - width if side else 0)
            wanted = (lane >= width * k) & (lane < width * (k + 1))
            tile = jnp.where(wanted, rolled(piece, shift, 1), tile)
        return tile

    for group in range(n):
        halos_out[0, group] = halo_tile(group, 0)

    mine = pl.ds(pl.multiple_of(px * nx, nx), nx)

    def block_copies(x):
        pieces = (
            (tracer_in.at[pl.ds(x * held, held)], blocks.at[:held, mine, :]),
            (metric_in, blocks.at[held:, mine, :]),
        )
        return [
            pltpu.make_async_remote_copy(
                src_ref=source,
                dst_ref=target,
                send_sem=block_send,
                recv_sem=block_recv,
                device_id=(x, py, lev),
                device_id_type=MESH,
            )
            for source, target in pieces
        ]

    def halo_copy(x, side):
        return pltpu.make_async_remote_copy(
            src_ref=halos_out.at[side, x],
            dst_ref=halos.at[side, mine, :],
            send_sem=halo_send.at[side],
            recv_sem=halo_recv.at[side],
            device_id=(x, py + (1 if side else -1), lev),
            device_id_type=MESH,
        )

    sides = ((0, has_low, has_high), (1, has_high, has_low))

    @pl.when(has_low)
    def _():
        for x in everyone:
            halo_copy(x, 0).start()

    for x in others():
        for copy in block_copies(x):
            copy.start()

    for group in range(n):
        halos_out[1, group] = halo_tile(group, 1)

    @pl.when(has_high)
    def _():
        pl.semaphore_wait(ready, n)
        for x in everyone:
            halo_copy(x, 1).start()

    blocks[:held, mine, :] = tracer_in[pl.ds(px * held, held)]
    blocks[held:, mine, :] = metric_in[...]
    for side, _, gets in sides:

        @pl.when(jnp.logical_not(gets))
        def _(side=side):
            halos[side] = jnp.zeros(halos.shape[1:], jnp.float32)

    def node_of(shape, axis):
        return lax.broadcasted_iota(jnp.int32, shape, axis)

    depth = ny + halos.shape[2]
    source = node_of((depth, 1), 0)
    slot = jnp.where(
        source < ny + width,
        reach + source // GLL_NODES,
        jnp.where(source < ny + 2 * width, (source - ny - width) // GLL_NODES, -SLOTS * GLL_NODES),
    )
    place = lax.rem(source, GLL_NODES) * SLOTS + slot
    column = node_of((1, spread.shape[1]), 1)
    spread[...] = jnp.where(place == column, 1.0, 0.0).astype(jnp.bfloat16)
    source = node_of((gather.shape[0], 1), 0)
    at = lax.rem(source, lanes)
    element = lax.rem(at, SLOTS) - reach
    kept = (element >= 0) & (element < elements_y) & (at // SLOTS < held)
    place = jnp.where(
        kept, at // SLOTS * ny + element * GLL_NODES + source // lanes, -1
    )
    gather[...] = jnp.where(place == node_of((1, gather.shape[1]), 1), 1.0, 0.0).astype(
        jnp.bfloat16
    )

    for side, _, gets in sides:

        @pl.when(gets)
        def _(side=side):
            took(halos.at[side], halo_recv.at[side])

    lane = lax.broadcasted_iota(jnp.int32, (elements_x, halos.shape[2]), 1)
    rows_of = [pl.ds(i, elements_x, stride=GLL_NODES) for i in range(GLL_NODES)]
    rims = []
    for rows in rows_of:
        high, low = halos[0, rows, :], halos[1, rows, :]
        rims.append(
            [
                jnp.where(
                    lane < width,
                    rolled(high, -width * k, 1),
                    jnp.where(lane < 2 * width, rolled(low, width - width * k, 1), 0.0),
                )
                for k in range(fields)
            ]
        )

    took(blocks.at[:, : (n - 1) * nx, :], block_recv)

    parts = [
        jnp.concatenate([blocks[k, rows_of[i], :], rims[i][k]], axis=1)
        for k in range(fields)
        for i in range(GLL_NODES)
    ]
    spread_out = moved_by_table(jnp.concatenate(parts, axis=0), spread[...])
    pair = 2 * SLOTS
    in_first = lax.broadcasted_iota(jnp.int32, (elements_x, pair), 1) < SLOTS

    def joined(first, second, i, j):
        first, second = (
            spread_out[
                (k * GLL_NODES + i) * elements_x : (k * GLL_NODES + i + 1) * elements_x,
                j // 2 * pair : (j // 2 + 1) * pair,
            ]
            for k in (first, second)
        )
        if j % 2:
            first = rolled(first, SLOTS, 1)
        else:
            second = rolled(second, SLOTS, 1)
        return jnp.where(in_first, first, second)

    def by_node(pairs):
        return [
            [
                jnp.concatenate([joined(first, second, i, j) for first, second in pairs], axis=1)
                for j in range(GLL_NODES)
            ]
            for i in range(GLL_NODES)
        ]

    tracer = by_node([(k, min(k + 1, held - 1)) for k in range(0, held, 2)])
    node_mass, wind_x, wind_y = (
        by_node([(held + k, held + k)] * (lanes // pair)) for k in range(3)
    )

    slot = lax.rem(lax.broadcasted_iota(jnp.int32, (elements_x, lanes), 1), SLOTS)
    element = py * elements_y + slot - reach
    inside = (slot < elements_y + 2 * reach) & (element >= 0) & (element < nz * elements_y)
    evolved = sections(tracer, node_mass, wind_x, wind_y, inside)

    evolved = moved_by_table(
        jnp.concatenate([jnp.concatenate(row, axis=1) for row in evolved], axis=0), gather[...]
    )
    for k in range(held):
        for i in range(GLL_NODES):
            results_out[k, pl.ds(i, elements_x, stride=GLL_NODES), :] = evolved[
                i * elements_x : (i + 1) * elements_x, k * ny : (k + 1) * ny
            ]

    holder = lax.rem(px, half)
    is_mine = target_lev == lev

    def result_copy(x):
        return pltpu.make_async_remote_copy(
            src_ref=results_out.at[:, pl.ds(pl.multiple_of(x * nx, nx), nx), :],
            dst_ref=results.at[lev, pl.ds(holder * held, held)],
            send_sem=result_send,
            recv_sem=result_recv,
            device_id=(x, py, target_lev),
            device_id_type=MESH,
        )

    @pl.when(jnp.logical_not(is_mine))
    def _():
        for x in everyone:
            result_copy(x).start()
        took(results_out, result_recv)

    @pl.when(is_mine)
    def _():
        for x in others():
            result_copy(x).start()
        results[lev, pl.ds(holder * held, held)] = results_out[:, mine, :]
        took(results_out.at[:, : (n - 1) * nx, :], result_recv)

    remap_copy.wait()
    for a in range(nlev):
        total = remap[a, 0] * results[0]
        for b in range(1, nlev):
            total = total + remap[a, b] * results[b]
        out[a] = total

    took(blocks.at[:, : (n - 1) * nx, :], block_send)
    for side, sends, _ in sides:

        @pl.when(sends)
        def _(side=side):
            took(halos.at[side], halo_send.at[side])

    @pl.when(is_mine)
    def _():
        took(results_out.at[:, : (n - 1) * nx, :], result_send)

    @pl.when(jnp.logical_not(is_mine))
    def _():
        took(results_out, result_send)


def shards(n, nz, nlev, tracer, node_mass, wind_x, wind_y, remap):
    levels, tracers, nx, ny = tracer.shape
    held = tracers // n
    fields = held + 3
    reach = SECTION_REACH * len(section_weights)
    width = reach * GLL_NODES
    elements_y = ny // GLL_NODES
    if levels != 1 or tracers % n or n % nlev or nx % 8 or ny % 128:
        raise ValueError("unsupported split")
    if elements_y + 2 * reach > SLOTS or fields * width > 128 or width > ny:
        raise ValueError("unsupported block")
    lanes = -(-held * SLOTS // 128) * 128
    vmem, dma = pltpu.VMEM, pltpu.SemaphoreType.DMA
    f32 = jnp.float32
    anywhere = pl.BlockSpec(memory_space=pltpu.HBM)
    return pl.pallas_call(
        functools.partial(kernel, n, nz, nlev),
        out_shape=vmem((nlev, tracers // nlev, nx, ny), f32),
        in_specs=[anywhere] * 5,
        out_specs=pl.BlockSpec(memory_space=pltpu.VMEM),
        scratch_shapes=[
            vmem((tracers, nx, ny), f32),
            vmem((3, nx, ny), f32),
            pltpu.SMEM(remap.shape, f32),
            vmem((2, n, nx, 128), f32),
            vmem((fields, n * nx, ny), f32),
            vmem((2, n * nx, 128), f32),
            vmem((ny + 128, GLL_NODES * SLOTS), jnp.bfloat16),
            vmem((GLL_NODES * lanes, held * ny), jnp.bfloat16),
            vmem((held, n * nx, ny), f32),
            vmem((nlev, tracers // nlev, nx, ny), f32),
            dma((5,)),
            dma,
            dma,
            dma((2,)),
            dma((2,)),
            dma,
            dma,
            pltpu.SemaphoreType.REGULAR,
        ],
        compiler_params=pltpu.CompilerParams(
            collective_id=0, has_side_effects=True, vmem_limit_bytes=32 * 1024 * 1024
        ),
        name="limited_step",
    )(
        *(
            pltpu.with_memory_space_constraint(operand, pltpu.HBM)
            for operand in (tracer, node_mass, wind_x, wind_y, remap)
        )
    )


def solution(mesh):
    sizes = [mesh.shape[axis] for axis in ("px", "py", "lev")]
    in_specs = (
        P("lev", None, "px", "py"),
        P("lev", "px", "py"),
        P("lev", "px", "py"),
        P("lev", "px", "py"),
        P(),
    )
    out_specs = P(None, "lev", "px", "py")
    return jax.shard_map(
        functools.partial(shards, *sizes),
        mesh=mesh,
        in_specs=in_specs,
        out_specs=out_specs,
        check_vma=False,
    )
```

```python
import functools

import jax
import jax.numpy as jnp
import numpy as np
from jax import lax
from jax.experimental import pallas as pl
from jax.experimental.pallas import tpu as pltpu
from jax.sharding import PartitionSpec as P

GLL_NODES = 4
SECTION_REACH = 2
SLOTS = 64

sentinel = 1e30
step_size = 0.1
section_weights = ((0.0, 1.0), (0.75, 0.25), (1.0 / 3.0, 2.0 / 3.0))
MESH = pl.DeviceIdType.MESH


def derivative_table():
    points = np.array([-1.0, -(5.0 ** (-0.5)), 5.0 ** (-0.5), 1.0])
    number = points.shape[0]
    barycentric = np.array(
        [
            1.0
            / np.prod([points[outer] - points[inner] for inner in range(number) if inner != outer])
            for outer in range(number)
        ]
    )
    table = np.zeros((number, number))
    for outer in range(number):
        for inner in range(number):
            if inner != outer:
                table[outer, inner] = (
                    barycentric[inner] / barycentric[outer] / (points[outer] - points[inner])
                )
    for outer in range(number):
        table[outer, outer] = -np.sum(table[outer])
    return table


def rolled(values, shift, axis):
    size = values.shape[axis]
    shift %= size
    return pltpu.roll(values, shift, axis) if shift else values


def moved_by_table(values, table):
    rows = values.shape[0]
    high = values.astype(jnp.bfloat16)
    low = (values - high.astype(jnp.float32)).astype(jnp.bfloat16)
    terms = jnp.dot(
        jnp.concatenate([high, low], axis=0), table, preferred_element_type=jnp.float32
    )
    return terms[:rows] + terms[rows:]


def sections(tracer, node_mass, wind_x, wind_y, inside):
    nodes = range(GLL_NODES)
    table = step_size * derivative_table()

    def node_sums(values):
        first = [values[0][j] + rolled(values[3][j], 1, 0) for j in nodes]
        last = [values[3][j] + rolled(values[0][j], -1, 0) for j in nodes]
        values = [first, values[1], values[2], last]
        return [
            [row[0] + rolled(row[3], 1, 1), row[1], row[2], row[3] + rolled(row[0], -1, 1)]
            for row in values
        ]

    def tree(combine, items):
        while len(items) > 1:
            items = [combine(*items[i : i + 2]) for i in range(0, len(items), 2)]
        return items[0]

    def around(combine, values):
        for axis in (0, 1):
            values = combine(
                combine(values, rolled(values, 1, axis)), rolled(values, -1, axis)
            )
        return values

    inverse = [
        [1.0 / jnp.where(inside, entry, 1.0) for entry in row] for row in node_sums(node_mass)
    ]
    field = tracer
    for share_start, share_new in section_weights:
        flat = [field[i][j] for i in nodes for j in nodes]
        lower = around(jnp.minimum, jnp.where(inside, tree(jnp.minimum, flat), sentinel))
        upper = around(jnp.maximum, jnp.where(inside, tree(jnp.maximum, flat), -sentinel))
        flux_x = [[wind_x[i][j] * field[i][j] for j in nodes] for i in nodes]
        flux_y = [[wind_y[i][j] * field[i][j] for j in nodes] for i in nodes]
        weighted = []
        for i in nodes:
            row = []
            for j in nodes:
                slope_x = tree(jnp.add, [float(table[i, k]) * flux_x[k][j] for k in nodes])
                slope_y = tree(jnp.add, [float(table[j, k]) * flux_y[i][k] for k in nodes])
                moved = field[i][j] - (slope_x + slope_y)
                limited = jnp.minimum(jnp.maximum(moved, lower), upper)
                row.append(node_mass[i][j] * limited)
            weighted.append(row)
        summed = node_sums(weighted)
        field = [
            [
                share_new * (summed[i][j] * inverse[i][j])
                + (share_start * tracer[i][j] if share_start else 0.0)
                for j in nodes
            ]
            for i in nodes
        ]
    return field


def kernel(
    n,
    nz,
    nlev,
    tracer_hbm,
    mass_hbm,
    wind_x_hbm,
    wind_y_hbm,
    remap_hbm,
    out,
    tracer_in,
    metric_in,
    remap,
    halos_out,
    blocks,
    halos,
    spread,
    gather,
    results_out,
    results,
    in_sem,
    block_send,
    block_recv,
    halo_send,
    halo_recv,
    result_send,
    result_recv,
    ready,
):
    tracers, nx, ny = tracer_in.shape
    held = tracers // n
    fields = held + 3
    half = n // nlev
    reach = SECTION_REACH * len(section_weights)
    width = reach * GLL_NODES
    elements_y = ny // GLL_NODES
    elements_x = n * nx // GLL_NODES
    lanes = gather.shape[0] // GLL_NODES
    px, py, lev = lax.axis_index("px"), lax.axis_index("py"), lax.axis_index("lev")
    has_low, has_high = py > 0, py < nz - 1
    target_lev = px // half

    def others():
        return [d + (d >= px).astype(jnp.int32) for d in range(n - 1)]

    everyone = list(range(n))

    def took(ref, sem):
        pltpu.make_async_copy(ref, ref, sem).wait()

    copies = [pltpu.make_async_copy(tracer_hbm.at[0], tracer_in, in_sem.at[0])]
    for k, source in enumerate((mass_hbm, wind_x_hbm, wind_y_hbm)):
        copies.append(pltpu.make_async_copy(source.at[0], metric_in.at[k], in_sem.at[k + 1]))
    remap_copy = pltpu.make_async_copy(remap_hbm, remap, in_sem.at[4])
    for copy in copies:
        copy.start()

    barrier = pltpu.get_barrier_semaphore()

    def greet(x, y, level):
        pl.semaphore_signal(barrier, inc=1, device_id=(x, y, level), device_id_type=MESH)

    for x in others():
        greet(x, py, lev)
    for x in everyone:
        for step in range(1, nlev):
            greet(x, py, lax.rem(lev + step, nlev))

    @pl.when(has_high)
    def _():
        for x in everyone:
            greet(x, py + 1, lev)

    peers = n * nlev - 1
    pl.semaphore_wait(barrier, peers + n * has_low.astype(jnp.int32))

    @pl.when(has_low)
    def _():
        for x in everyone:
            pl.semaphore_signal(
                ready, inc=1, device_id=(x, py - 1, lev), device_id_type=MESH
            )

    remap_copy.start()
    for copy in copies:
        copy.wait()

    lane = lax.broadcasted_iota(jnp.int32, (nx, halos.shape[2]), 1)

    def halo_tile(group, side):
        tile = jnp.zeros(lane.shape, jnp.float32)
        for k in range(fields):
            piece = tracer_in[group * held + k] if k < held else metric_in[k - held]
            shift = width * k - (ny - width if side else 0)
            wanted = (lane >= width * k) & (lane < width * (k + 1))
            tile = jnp.where(wanted, rolled(piece, shift, 1), tile)
        return tile

    for group in range(n):
        halos_out[0, group] = halo_tile(group, 0)

    mine = pl.ds(pl.multiple_of(px * nx, nx), nx)

    def block_copies(x):
        pieces = (
            (tracer_in.at[pl.ds(x * held, held)], blocks.at[:held, mine, :]),
            (metric_in, blocks.at[held:, mine, :]),
        )
        return [
            pltpu.make_async_remote_copy(
                src_ref=source,
                dst_ref=target,
                send_sem=block_send,
                recv_sem=block_recv,
                device_id=(x, py, lev),
                device_id_type=MESH,
            )
            for source, target in pieces
        ]

    def halo_copy(x, side):
        return pltpu.make_async_remote_copy(
            src_ref=halos_out.at[side, x],
            dst_ref=halos.at[side, mine, :],
            send_sem=halo_send.at[side],
            recv_sem=halo_recv.at[side],
            device_id=(x, py + (1 if side else -1), lev),
            device_id_type=MESH,
        )

    sides = ((0, has_low, has_high), (1, has_high, has_low))

    @pl.when(has_low)
    def _():
        for x in everyone:
            halo_copy(x, 0).start()

    for x in others():
        for copy in block_copies(x):
            copy.start()

    for group in range(n):
        halos_out[1, group] = halo_tile(group, 1)

    @pl.when(has_high)
    def _():
        pl.semaphore_wait(ready, n)
        for x in everyone:
            halo_copy(x, 1).start()

    blocks[:held, mine, :] = tracer_in[pl.ds(px * held, held)]
    blocks[held:, mine, :] = metric_in[...]
    for side, _, gets in sides:

        @pl.when(jnp.logical_not(gets))
        def _(side=side):
            halos[side] = jnp.zeros(halos.shape[1:], jnp.float32)

    def node_of(shape, axis):
        return lax.broadcasted_iota(jnp.int32, shape, axis)

    depth = ny + halos.shape[2]
    source = node_of((depth, 1), 0)
    slot = jnp.where(
        source < ny + width,
        reach + source // GLL_NODES,
        jnp.where(source < ny + 2 * width, (source - ny - width) // GLL_NODES, -SLOTS * GLL_NODES),
    )
    place = lax.rem(source, GLL_NODES) * SLOTS + slot
    column = node_of((1, spread.shape[1]), 1)
    spread[...] = jnp.where(place == column, 1.0, 0.0).astype(jnp.bfloat16)
    source = node_of((gather.shape[0], 1), 0)
    at = lax.rem(source, lanes)
    element = lax.rem(at, SLOTS) - reach
    kept = (element >= 0) & (element < elements_y) & (at // SLOTS < held)
    place = jnp.where(
        kept, at // SLOTS * ny + element * GLL_NODES + source // lanes, -1
    )
    gather[...] = jnp.where(place == node_of((1, gather.shape[1]), 1), 1.0, 0.0).astype(
        jnp.bfloat16
    )

    for side, _, gets in sides:

        @pl.when(gets)
        def _(side=side):
            took(halos.at[side], halo_recv.at[side])

    lane = lax.broadcasted_iota(jnp.int32, (elements_x, halos.shape[2]), 1)
    rows_of = [pl.ds(i, elements_x, stride=GLL_NODES) for i in range(GLL_NODES)]
    rims = []
    for rows in rows_of:
        high, low = halos[0, rows, :], halos[1, rows, :]
        rims.append(
            [
                jnp.where(
                    lane < width,
                    rolled(high, -width * k, 1),
                    jnp.where(lane < 2 * width, rolled(low, width - width * k, 1), 0.0),
                )
                for k in range(fields)
            ]
        )

    took(blocks.at[:, : (n - 1) * nx, :], block_recv)

    parts = [
        jnp.concatenate([blocks[k, rows_of[i], :], rims[i][k]], axis=1)
        for k in range(fields)
        for i in range(GLL_NODES)
    ]
    table = spread[...]
    cut = held * GLL_NODES
    spread_out = [
        moved_by_table(jnp.concatenate(group, axis=0), table) for group in (parts[:cut], parts[cut:])
    ]
    pair = 2 * SLOTS
    in_first = lax.broadcasted_iota(jnp.int32, (elements_x, pair), 1) < SLOTS

    def joined(first, second, i, j):
        def piece(k):
            values, at = (spread_out[0], k) if k < held else (spread_out[1], k - held)
            start = (at * GLL_NODES + i) * elements_x
            return values[start : start + elements_x, j // 2 * pair : (j // 2 + 1) * pair]

        first, second = piece(first), piece(second)
        if j % 2:
            first = rolled(first, SLOTS, 1)
        else:
            second = rolled(second, SLOTS, 1)
        return jnp.where(in_first, first, second)

    def by_node(pairs):
        return [
            [
                jnp.concatenate([joined(first, second, i, j) for first, second in pairs], axis=1)
                for j in range(GLL_NODES)
            ]
            for i in range(GLL_NODES)
        ]

    tracer = by_node([(k, min(k + 1, held - 1)) for k in range(0, held, 2)])
    node_mass, wind_x, wind_y = (
        by_node([(held + k, held + k)] * (lanes // pair)) for k in range(3)
    )

    slot = lax.rem(lax.broadcasted_iota(jnp.int32, (elements_x, lanes), 1), SLOTS)
    element = py * elements_y + slot - reach
    inside = (slot < elements_y + 2 * reach) & (element >= 0) & (element < nz * elements_y)
    evolved = sections(tracer, node_mass, wind_x, wind_y, inside)

    evolved = moved_by_table(
        jnp.concatenate([jnp.concatenate(row, axis=1) for row in evolved], axis=0), gather[...]
    )
    for k in range(held):
        for i in range(GLL_NODES):
            results_out[k, pl.ds(i, elements_x, stride=GLL_NODES), :] = evolved[
                i * elements_x : (i + 1) * elements_x, k * ny : (k + 1) * ny
            ]

    holder = lax.rem(px, half)
    is_mine = target_lev == lev

    def result_copy(x):
        return pltpu.make_async_remote_copy(
            src_ref=results_out.at[:, pl.ds(pl.multiple_of(x * nx, nx), nx), :],
            dst_ref=results.at[lev, pl.ds(holder * held, held)],
            send_sem=result_send,
            recv_sem=result_recv,
            device_id=(x, py, target_lev),
            device_id_type=MESH,
        )

    @pl.when(jnp.logical_not(is_mine))
    def _():
        for x in everyone:
            result_copy(x).start()
        took(results_out, result_recv)

    @pl.when(is_mine)
    def _():
        for x in others():
            result_copy(x).start()
        results[lev, pl.ds(holder * held, held)] = results_out[:, mine, :]
        took(results_out.at[:, : (n - 1) * nx, :], result_recv)

    remap_copy.wait()
    for a in range(nlev):
        total = remap[a, 0] * results[0]
        for b in range(1, nlev):
            total = total + remap[a, b] * results[b]
        out[a] = total

    took(blocks.at[:, : (n - 1) * nx, :], block_send)
    for side, sends, _ in sides:

        @pl.when(sends)
        def _(side=side):
            took(halos.at[side], halo_send.at[side])

    @pl.when(is_mine)
    def _():
        took(results_out.at[:, : (n - 1) * nx, :], result_send)

    @pl.when(jnp.logical_not(is_mine))
    def _():
        took(results_out, result_send)


def shards(n, nz, nlev, tracer, node_mass, wind_x, wind_y, remap):
    levels, tracers, nx, ny = tracer.shape
    held = tracers // n
    fields = held + 3
    reach = SECTION_REACH * len(section_weights)
    width = reach * GLL_NODES
    elements_y = ny // GLL_NODES
    if levels != 1 or tracers % n or n % nlev or nx % 8 or ny % 128:
        raise ValueError("unsupported split")
    if elements_y + 2 * reach > SLOTS or fields * width > 128 or width > ny:
        raise ValueError("unsupported block")
    lanes = -(-held * SLOTS // 128) * 128
    vmem, dma = pltpu.VMEM, pltpu.SemaphoreType.DMA
    f32 = jnp.float32
    anywhere = pl.BlockSpec(memory_space=pltpu.HBM)
    return pl.pallas_call(
        functools.partial(kernel, n, nz, nlev),
        out_shape=vmem((nlev, tracers // nlev, nx, ny), f32),
        in_specs=[anywhere] * 5,
        out_specs=pl.BlockSpec(memory_space=pltpu.VMEM),
        scratch_shapes=[
            vmem((tracers, nx, ny), f32),
            vmem((3, nx, ny), f32),
            pltpu.SMEM(remap.shape, f32),
            vmem((2, n, nx, 128), f32),
            vmem((fields, n * nx, ny), f32),
            vmem((2, n * nx, 128), f32),
            vmem((ny + 128, GLL_NODES * SLOTS), jnp.bfloat16),
            vmem((GLL_NODES * lanes, held * ny), jnp.bfloat16),
            vmem((held, n * nx, ny), f32),
            vmem((nlev, tracers // nlev, nx, ny), f32),
            dma((5,)),
            dma,
            dma,
            dma((2,)),
            dma((2,)),
            dma,
            dma,
            pltpu.SemaphoreType.REGULAR,
        ],
        compiler_params=pltpu.CompilerParams(
            collective_id=0, has_side_effects=True, vmem_limit_bytes=32 * 1024 * 1024
        ),
        name="limited_step",
    )(
        *(
            pltpu.with_memory_space_constraint(operand, pltpu.HBM)
            for operand in (tracer, node_mass, wind_x, wind_y, remap)
        )
    )


def solution(mesh):
    sizes = [mesh.shape[axis] for axis in ("px", "py", "lev")]
    in_specs = (
        P("lev", None, "px", "py"),
        P("lev", "px", "py"),
        P("lev", "px", "py"),
        P("lev", "px", "py"),
        P(),
    )
    out_specs = P(None, "lev", "px", "py")
    return jax.shard_map(
        functools.partial(shards, *sizes),
        mesh=mesh,
        in_specs=in_specs,
        out_specs=out_specs,
        check_vma=False,
    )
```

```python
import functools

import jax
import jax.numpy as jnp
import numpy as np
from jax import lax
from jax.experimental import pallas as pl
from jax.experimental.pallas import tpu as pltpu
from jax.sharding import PartitionSpec as P

GLL_NODES = 4
SECTION_REACH = 2
SLOTS = 64

sentinel = 1e30
step_size = 0.1
section_weights = ((0.0, 1.0), (0.75, 0.25), (1.0 / 3.0, 2.0 / 3.0))
MESH = pl.DeviceIdType.MESH


def derivative_table():
    points = np.array([-1.0, -(5.0 ** (-0.5)), 5.0 ** (-0.5), 1.0])
    number = points.shape[0]
    barycentric = np.array(
        [
            1.0
            / np.prod([points[outer] - points[inner] for inner in range(number) if inner != outer])
            for outer in range(number)
        ]
    )
    table = np.zeros((number, number))
    for outer in range(number):
        for inner in range(number):
            if inner != outer:
                table[outer, inner] = (
                    barycentric[inner] / barycentric[outer] / (points[outer] - points[inner])
                )
    for outer in range(number):
        table[outer, outer] = -np.sum(table[outer])
    return table


def rolled(values, shift, axis):
    size = values.shape[axis]
    shift %= size
    return pltpu.roll(values, shift, axis) if shift else values


def moved_by_table(values, table):
    rows = values.shape[0]
    high = values.astype(jnp.bfloat16)
    low = (values - high.astype(jnp.float32)).astype(jnp.bfloat16)
    terms = jnp.dot(
        jnp.concatenate([high, low], axis=0), table, preferred_element_type=jnp.float32
    )
    return terms[:rows] + terms[rows:]


def sections(tracer, node_mass, wind_x, wind_y, inside):
    nodes = range(GLL_NODES)
    table = step_size * derivative_table()

    def node_sums(values):
        first = [values[0][j] + rolled(values[3][j], 1, 0) for j in nodes]
        last = [values[3][j] + rolled(values[0][j], -1, 0) for j in nodes]
        values = [first, values[1], values[2], last]
        return [
            [row[0] + rolled(row[3], 1, 1), row[1], row[2], row[3] + rolled(row[0], -1, 1)]
            for row in values
        ]

    def tree(combine, items):
        while len(items) > 1:
            items = [combine(*items[i : i + 2]) for i in range(0, len(items), 2)]
        return items[0]

    def around(combine, values):
        for axis in (0, 1):
            values = combine(
                combine(values, rolled(values, 1, axis)), rolled(values, -1, axis)
            )
        return values

    inverse = [
        [1.0 / jnp.where(inside, entry, 1.0) for entry in row] for row in node_sums(node_mass)
    ]
    field = tracer
    for share_start, share_new in section_weights:
        flat = [field[i][j] for i in nodes for j in nodes]
        lower = around(jnp.minimum, jnp.where(inside, tree(jnp.minimum, flat), sentinel))
        upper = around(jnp.maximum, jnp.where(inside, tree(jnp.maximum, flat), -sentinel))
        flux_x = [[wind_x[i][j] * field[i][j] for j in nodes] for i in nodes]
        flux_y = [[wind_y[i][j] * field[i][j] for j in nodes] for i in nodes]
        weighted = []
        for i in nodes:
            row = []
            for j in nodes:
                slope_x = tree(jnp.add, [float(table[i, k]) * flux_x[k][j] for k in nodes])
                slope_y = tree(jnp.add, [float(table[j, k]) * flux_y[i][k] for k in nodes])
                moved = field[i][j] - (slope_x + slope_y)
                limited = jnp.minimum(jnp.maximum(moved, lower), upper)
                row.append(node_mass[i][j] * limited)
            weighted.append(row)
        summed = node_sums(weighted)
        field = [
            [
                share_new * (summed[i][j] * inverse[i][j])
                + (share_start * tracer[i][j] if share_start else 0.0)
                for j in nodes
            ]
            for i in nodes
        ]
    return field


def kernel(
    n,
    nz,
    nlev,
    tracer_hbm,
    mass_hbm,
    wind_x_hbm,
    wind_y_hbm,
    remap_hbm,
    out,
    tracer_in,
    metric_in,
    remap,
    halos_out,
    blocks,
    halos,
    spread,
    gather,
    results_out,
    results,
    in_sem,
    block_send,
    block_recv,
    halo_send,
    halo_recv,
    result_send,
    result_recv,
    ready,
):
    tracers, nx, ny = tracer_in.shape
    held = tracers // n
    fields = held + 3
    half = n // nlev
    reach = SECTION_REACH * len(section_weights)
    width = reach * GLL_NODES
    elements_y = ny // GLL_NODES
    elements_x = n * nx // GLL_NODES
    lanes = gather.shape[0] // GLL_NODES
    px, py, lev = lax.axis_index("px"), lax.axis_index("py"), lax.axis_index("lev")
    has_low, has_high = py > 0, py < nz - 1
    target_lev = px // half

    def others():
        return [d + (d >= px).astype(jnp.int32) for d in range(n - 1)]

    everyone = list(range(n))

    def took(ref, sem):
        pltpu.make_async_copy(ref, ref, sem).wait()

    copies = [pltpu.make_async_copy(tracer_hbm.at[0], tracer_in, in_sem.at[0])]
    for k, source in enumerate((mass_hbm, wind_x_hbm, wind_y_hbm)):
        copies.append(pltpu.make_async_copy(source.at[0], metric_in.at[k], in_sem.at[k + 1]))
    remap_copy = pltpu.make_async_copy(remap_hbm, remap, in_sem.at[4])
    for copy in copies:
        copy.start()

    barrier = pltpu.get_barrier_semaphore()

    def greet(x, y, level):
        pl.semaphore_signal(barrier, inc=1, device_id=(x, y, level), device_id_type=MESH)

    for x in others():
        greet(x, py, lev)
    for x in everyone:
        for step in range(1, nlev):
            greet(x, py, lax.rem(lev + step, nlev))

    @pl.when(has_high)
    def _():
        for x in everyone:
            greet(x, py + 1, lev)

    peers = n * nlev - 1
    pl.semaphore_wait(barrier, peers + n * has_low.astype(jnp.int32))

    @pl.when(has_low)
    def _():
        for x in everyone:
            pl.semaphore_signal(
                ready, inc=1, device_id=(x, py - 1, lev), device_id_type=MESH
            )

    mine = pl.ds(pl.multiple_of(px * nx, nx), nx)

    def block_copies(x):
        pieces = (
            (tracer_hbm.at[0, pl.ds(x * held, held)], blocks.at[:held, mine, :]),
            (mass_hbm.at[0], blocks.at[held, mine, :]),
            (wind_x_hbm.at[0], blocks.at[held + 1, mine, :]),
            (wind_y_hbm.at[0], blocks.at[held + 2, mine, :]),
        )
        return [
            pltpu.make_async_remote_copy(
                src_ref=source,
                dst_ref=target,
                send_sem=block_send,
                recv_sem=block_recv,
                device_id=(x, py, lev),
                device_id_type=MESH,
            )
            for source, target in pieces
        ]

    for x in others():
        for copy in block_copies(x):
            copy.start()

    remap_copy.start()
    for copy in copies:
        copy.wait()

    lane = lax.broadcasted_iota(jnp.int32, (nx, halos.shape[2]), 1)

    def halo_tile(group, side):
        tile = jnp.zeros(lane.shape, jnp.float32)
        for k in range(fields):
            piece = tracer_in[group * held + k] if k < held else metric_in[k - held]
            shift = width * k - (ny - width if side else 0)
            wanted = (lane >= width * k) & (lane < width * (k + 1))
            tile = jnp.where(wanted, rolled(piece, shift, 1), tile)
        return tile

    for group in range(n):
        halos_out[0, group] = halo_tile(group, 0)

    def halo_copy(x, side):
        return pltpu.make_async_remote_copy(
            src_ref=halos_out.at[side, x],
            dst_ref=halos.at[side, mine, :],
            send_sem=halo_send.at[side],
            recv_sem=halo_recv.at[side],
            device_id=(x, py + (1 if side else -1), lev),
            device_id_type=MESH,
        )

    sides = ((0, has_low, has_high), (1, has_high, has_low))

    @pl.when(has_low)
    def _():
        for x in everyone:
            halo_copy(x, 0).start()

    for group in range(n):
        halos_out[1, group] = halo_tile(group, 1)

    @pl.when(has_high)
    def _():
        pl.semaphore_wait(ready, n)
        for x in everyone:
            halo_copy(x, 1).start()

    blocks[:held, mine, :] = tracer_in[pl.ds(px * held, held)]
    blocks[held:, mine, :] = metric_in[...]
    for side, _, gets in sides:

        @pl.when(jnp.logical_not(gets))
        def _(side=side):
            halos[side] = jnp.zeros(halos.shape[1:], jnp.float32)

    def node_of(shape, axis):
        return lax.broadcasted_iota(jnp.int32, shape, axis)

    depth = ny + halos.shape[2]
    source = node_of((depth, 1), 0)
    slot = jnp.where(
        source < ny + width,
        reach + source // GLL_NODES,
        jnp.where(source < ny + 2 * width, (source - ny - width) // GLL_NODES, -SLOTS * GLL_NODES),
    )
    place = lax.rem(source, GLL_NODES) * SLOTS + slot
    column = node_of((1, spread.shape[1]), 1)
    spread[...] = jnp.where(place == column, 1.0, 0.0).astype(jnp.bfloat16)
    source = node_of((gather.shape[0], 1), 0)
    at = lax.rem(source, lanes)
    element = lax.rem(at, SLOTS) - reach
    kept = (element >= 0) & (element < elements_y) & (at // SLOTS < held)
    place = jnp.where(
        kept, at // SLOTS * ny + element * GLL_NODES + source // lanes, -1
    )
    gather[...] = jnp.where(place == node_of((1, gather.shape[1]), 1), 1.0, 0.0).astype(
        jnp.bfloat16
    )

    for side, _, gets in sides:

        @pl.when(gets)
        def _(side=side):
            took(halos.at[side], halo_recv.at[side])

    lane = lax.broadcasted_iota(jnp.int32, (elements_x, halos.shape[2]), 1)
    rows_of = [pl.ds(i, elements_x, stride=GLL_NODES) for i in range(GLL_NODES)]
    rims = []
    for rows in rows_of:
        high, low = halos[0, rows, :], halos[1, rows, :]
        rims.append(
            [
                jnp.where(
                    lane < width,
                    rolled(high, -width * k, 1),
                    jnp.where(lane < 2 * width, rolled(low, width - width * k, 1), 0.0),
                )
                for k in range(fields)
            ]
        )

    took(blocks.at[:, : (n - 1) * nx, :], block_recv)

    parts = [
        jnp.concatenate([blocks[k, rows_of[i], :], rims[i][k]], axis=1)
        for k in range(fields)
        for i in range(GLL_NODES)
    ]
    table = spread[...]
    cut = held * GLL_NODES
    spread_out = [
        moved_by_table(jnp.concatenate(group, axis=0), table) for group in (parts[:cut], parts[cut:])
    ]
    pair = 2 * SLOTS
    in_first = lax.broadcasted_iota(jnp.int32, (elements_x, pair), 1) < SLOTS

    def joined(first, second, i, j):
        def piece(k):
            values, at = (spread_out[0], k) if k < held else (spread_out[1], k - held)
            start = (at * GLL_NODES + i) * elements_x
            return values[start : start + elements_x, j // 2 * pair : (j // 2 + 1) * pair]

        first, second = piece(first), piece(second)
        if j % 2:
            first = rolled(first, SLOTS, 1)
        else:
            second = rolled(second, SLOTS, 1)
        return jnp.where(in_first, first, second)

    def by_node(pairs):
        return [
            [
                jnp.concatenate([joined(first, second, i, j) for first, second in pairs], axis=1)
                for j in range(GLL_NODES)
            ]
            for i in range(GLL_NODES)
        ]

    tracer = by_node([(k, min(k + 1, held - 1)) for k in range(0, held, 2)])
    node_mass, wind_x, wind_y = (
        by_node([(held + k, held + k)] * (lanes // pair)) for k in range(3)
    )

    slot = lax.rem(lax.broadcasted_iota(jnp.int32, (elements_x, lanes), 1), SLOTS)
    element = py * elements_y + slot - reach
    inside = (slot < elements_y + 2 * reach) & (element >= 0) & (element < nz * elements_y)
    evolved = sections(tracer, node_mass, wind_x, wind_y, inside)

    evolved = moved_by_table(
        jnp.concatenate([jnp.concatenate(row, axis=1) for row in evolved], axis=0), gather[...]
    )
    for k in range(held):
        for i in range(GLL_NODES):
            results_out[k, pl.ds(i, elements_x, stride=GLL_NODES), :] = evolved[
                i * elements_x : (i + 1) * elements_x, k * ny : (k + 1) * ny
            ]

    holder = lax.rem(px, half)
    is_mine = target_lev == lev

    def result_copy(x):
        return pltpu.make_async_remote_copy(
            src_ref=results_out.at[:, pl.ds(pl.multiple_of(x * nx, nx), nx), :],
            dst_ref=results.at[lev, pl.ds(holder * held, held)],
            send_sem=result_send,
            recv_sem=result_recv,
            device_id=(x, py, target_lev),
            device_id_type=MESH,
        )

    @pl.when(jnp.logical_not(is_mine))
    def _():
        for x in everyone:
            result_copy(x).start()
        took(results_out, result_recv)

    @pl.when(is_mine)
    def _():
        for x in others():
            result_copy(x).start()
        results[lev, pl.ds(holder * held, held)] = results_out[:, mine, :]
        took(results_out.at[:, : (n - 1) * nx, :], result_recv)

    remap_copy.wait()
    for a in range(nlev):
        total = remap[a, 0] * results[0]
        for b in range(1, nlev):
            total = total + remap[a, b] * results[b]
        out[a] = total

    took(blocks.at[:, : (n - 1) * nx, :], block_send)
    for side, sends, _ in sides:

        @pl.when(sends)
        def _(side=side):
            took(halos.at[side], halo_send.at[side])

    @pl.when(is_mine)
    def _():
        took(results_out.at[:, : (n - 1) * nx, :], result_send)

    @pl.when(jnp.logical_not(is_mine))
    def _():
        took(results_out, result_send)


def shards(n, nz, nlev, tracer, node_mass, wind_x, wind_y, remap):
    levels, tracers, nx, ny = tracer.shape
    held = tracers // n
    fields = held + 3
    reach = SECTION_REACH * len(section_weights)
    width = reach * GLL_NODES
    elements_y = ny // GLL_NODES
    if levels != 1 or tracers % n or n % nlev or nx % 8 or ny % 128:
        raise ValueError("unsupported split")
    if elements_y + 2 * reach > SLOTS or fields * width > 128 or width > ny:
        raise ValueError("unsupported block")
    lanes = -(-held * SLOTS // 128) * 128
    vmem, dma = pltpu.VMEM, pltpu.SemaphoreType.DMA
    f32 = jnp.float32
    anywhere = pl.BlockSpec(memory_space=pltpu.HBM)
    return pl.pallas_call(
        functools.partial(kernel, n, nz, nlev),
        out_shape=vmem((nlev, tracers // nlev, nx, ny), f32),
        in_specs=[anywhere] * 5,
        out_specs=pl.BlockSpec(memory_space=pltpu.VMEM),
        scratch_shapes=[
            vmem((tracers, nx, ny), f32),
            vmem((3, nx, ny), f32),
            pltpu.SMEM(remap.shape, f32),
            vmem((2, n, nx, 128), f32),
            vmem((fields, n * nx, ny), f32),
            vmem((2, n * nx, 128), f32),
            vmem((ny + 128, GLL_NODES * SLOTS), jnp.bfloat16),
            vmem((GLL_NODES * lanes, held * ny), jnp.bfloat16),
            vmem((held, n * nx, ny), f32),
            vmem((nlev, tracers // nlev, nx, ny), f32),
            dma((5,)),
            dma,
            dma,
            dma((2,)),
            dma((2,)),
            dma,
            dma,
            pltpu.SemaphoreType.REGULAR,
        ],
        compiler_params=pltpu.CompilerParams(
            collective_id=0, has_side_effects=True, vmem_limit_bytes=32 * 1024 * 1024
        ),
        name="limited_step",
    )(
        *(
            pltpu.with_memory_space_constraint(operand, pltpu.HBM)
            for operand in (tracer, node_mass, wind_x, wind_y, remap)
        )
    )


def solution(mesh):
    sizes = [mesh.shape[axis] for axis in ("px", "py", "lev")]
    in_specs = (
        P("lev", None, "px", "py"),
        P("lev", "px", "py"),
        P("lev", "px", "py"),
        P("lev", "px", "py"),
        P(),
    )
    out_specs = P(None, "lev", "px", "py")
    return jax.shard_map(
        functools.partial(shards, *sizes),
        mesh=mesh,
        in_specs=in_specs,
        out_specs=out_specs,
        check_vma=False,
    )
```
